512 devices in a mesh: layer: 8 (over z), dom: 64 (over x, y, core).
Axes of the slice: x: 4, y: 8, z: 8, core: 2. Of those that a mesh axis runs over, the one named last changes fastest.
Arguments:
- features: bfloat16 [2, 16384, 256], P(None, 'dom'), may hold values from -6 to 6
- weight: bfloat16 [8, 256, 256], P('layer'), may hold values from -0.375 to 0.375
- bias: float32 [8, 256], P('layer'), may hold values from -3 to 3
- gain: float32 [8, 256], P('layer'), may hold values from 0.5 to 1.5
- tile_col: int32 [2, 128, 4], P(None, 'dom'), may hold values from 0 to 1
- tile_adj: int32 [2, 128, 4, 128, 128], P(None, 'dom'), may hold values 0 or 1
- send_rows: int32 [2, 64, 64, 8], P(None, 'dom'), may hold values from 0 to 255
- recv_dst: int32 [2, 64, 64, 8], P(None, 'dom'), may hold values from -1 to 255, as said below
Outputs:
- layer_states: bfloat16 [8, 2, 16384, 256], P('layer', None, 'dom')
The draws below stay inside these ranges and needn't reach their ends.
Inputs may be any that keep to these rules, and one draw needn't show every extreme that they name: `recv_dst`: no partition has slots from itself (all -1). From every other sender either no slot or all 8 slots are live; every receiver has at least one sender whose 8 slots are all live.
All inputs are finite; a program needn't handle non-finite values. No bound on the sum of `tile_adj` on one device may be relied on, other than what follows from the above.
Results may differ from the reference program's by a relative error of at most 0.02.
Values may be sent and summed in bfloat16 or wider, within the bound.
No kernel may reach another device: no remote copies, remote signals or barrier semaphores. Data moves between devices by JAX's collectives and lax.ppermute only.
A program may use at most 64 MiB of HBM per device.

```python
import jax
import jax.numpy as jnp
from jax import lax

D = 256
ROWS = 256
SPANS = 2
TILE = 128
KT = 4
BMAX = 8
LAYERS = 8
NODES = 16384
N_LAYER = 8
N_DOM = 64


def draw_recv_dst(key, part):
    key = jax.random.fold_in(key, 11)
    first, second, third = jax.random.split(key, 3)
    live_pick = jax.random.randint(first, (SPANS, N_DOM, N_DOM), 0, 4)
    counts = jnp.where(live_pick > 0, BMAX, 0)
    offset = jax.random.randint(second, (SPANS, N_DOM, 1), 1, N_DOM)
    receiver = jnp.arange(N_DOM)[None, :, None]
    sender = jnp.arange(N_DOM)[None, None, :]
    counts = jnp.where(sender == (receiver + offset) % N_DOM, BMAX, counts)
    counts = jnp.where(sender == receiver, 0, counts)
    row_ids = jax.random.randint(third, (SPANS, N_DOM, N_DOM, BMAX), 0, ROWS)
    slots = jnp.arange(BMAX)
    return jnp.where(slots < counts[..., None], row_ids, -1).astype(jnp.int32)


def draw_weight(key, part):
    key = jax.random.fold_in(key, 23)
    first, second, third = jax.random.split(key, 3)
    row_sign = (2 * jax.random.randint(first, (LAYERS, D, 1), 0, 2) - 1).astype(jnp.float32)
    col_sign = (2 * jax.random.randint(second, (LAYERS, 1, D), 0, 2) - 1).astype(jnp.float32)
    index_row = jnp.arange(D, dtype=jnp.int32)[:, None]
    index_col = jnp.arange(D, dtype=jnp.int32)[None, :]
    intersection = jnp.bitwise_and(index_row, index_col)
    parity = jnp.zeros((D, D), jnp.int32)
    for bit_now in range(16):
        parity = jnp.bitwise_xor(parity, jnp.bitwise_and(jnp.right_shift(intersection, bit_now), 1))
    hadamard = 1.0 - 2.0 * parity.astype(jnp.float32)
    noise = jnp.clip(jax.random.normal(third, (LAYERS, D, D), jnp.float32), -1.5, 1.5)
    signed = row_sign * hadamard[None, :, :] * col_sign
    return (0.22 * signed + 0.1 * noise).astype(jnp.bfloat16)


def plant(array, stream_key, low, largest):
    shape = array.shape
    index_at = [jax.random.randint(jax.random.fold_in(stream_key, axis), (), 0, shape[axis]) for axis in range(len(shape))]
    array = array.at[tuple(index_at)].set(low)
    longest = shape.index(max(shape))
    index_at[longest] = (index_at[longest] + 1) % shape[longest]
    return array.at[tuple(index_at)].set(largest)


def block_levels(own_key, dims, cuts, low, high):
    level = 1.0
    for dim, shards_of in cuts:
        steps = jax.random.uniform(jax.random.fold_in(jax.random.fold_in(own_key, 6), dim), (shards_of,), jnp.float32, low / len(cuts), high / len(cuts))
        level = level * jnp.repeat(jnp.exp(steps), dims[dim] // shards_of).reshape((-1,) + (1,) * (len(dims) - 1 - dim))
    return level


def bell_draw(rng, shape, scale, limit, cuts=(), kind=jnp.bfloat16):
    array = scale * jax.random.normal(rng, shape, jnp.float32)
    if cuts:
        array = array * block_levels(rng, shape, cuts, -0.22, 0.18)
    return jnp.clip(array, -limit, limit).astype(kind)


def setup_inputs(seed: int = 0) -> dict:
    streams_of = jax.random.split(jax.random.key(seed), 9)
    return {
        "features": bell_draw(streams_of[0], (SPANS, NODES, D), 1.0, 6.0, ((1, 64),)),
        "weight": draw_weight(jax.random.fold_in(streams_of[8], 71), 0),
        "bias": bell_draw(streams_of[2], (LAYERS, D), 0.5, 3.0, ((0, 8),), jnp.float32),
        "gain": jnp.clip(1.0 + 0.1 * jax.random.normal(streams_of[3], (LAYERS, D), jnp.float32), 0.5, 1.5),
        "tile_col": plant(jax.random.randint(streams_of[4], (SPANS, NODES // TILE, KT), 0, ROWS // TILE), jax.random.fold_in(streams_of[4], 1), 0, (ROWS // TILE) - 1).astype(jnp.int32),
        "tile_adj": plant((jax.random.randint(streams_of[5], (SPANS, NODES // TILE, KT, TILE, TILE), 0, KT * TILE) < 1).astype(jnp.int32), jax.random.fold_in(streams_of[5], 1), 0, 1),
        "send_rows": plant(jax.random.randint(streams_of[6], (SPANS, N_DOM, N_DOM, BMAX), 0, ROWS), jax.random.fold_in(streams_of[6], 1), 0, ROWS - 1).astype(jnp.int32),
        "recv_dst": draw_recv_dst(jax.random.fold_in(streams_of[8], 71), 0),
    }


def apply_layer(hidden, tile_cols, adjacency, send_list, dest_rows, layer_weight, layer_bias, layer_gain):
    partitions = hidden.reshape(N_DOM, ROWS, D)
    row_blocks = ROWS // TILE
    blocks = partitions.reshape(N_DOM, row_blocks, TILE, D)
    cols_all = tile_cols.reshape(N_DOM, row_blocks, KT)
    adj_all = adjacency.reshape(N_DOM, row_blocks, KT, TILE, TILE)

    def local_one(packed):
        block_rows, columns, tiles = packed
        picked = block_rows[columns].astype(jnp.float32)
        return jnp.einsum('rkij,rkjd->rid', tiles.astype(jnp.float32), picked)
    local_sum = lax.map(local_one, (blocks, cols_all, adj_all)).reshape(N_DOM, ROWS, D)
    local_degree = lax.optimization_barrier(jnp.sum(adj_all, axis=(2, 4))).astype(jnp.float32).reshape(N_DOM, ROWS)
    senders = jnp.arange(N_DOM)[:, None, None]
    arrived = partitions[senders, send_list]
    targets = jnp.transpose(dest_rows, (1, 0, 2))
    live_mask = targets >= 0
    safe_rows = jnp.where(live_mask, targets, 0).astype(jnp.int32)
    owners = jnp.broadcast_to(jnp.arange(N_DOM)[None, :, None], targets.shape)
    weighted = arrived.astype(jnp.float32) * live_mask[..., None].astype(jnp.float32)
    boundary_sum = jnp.zeros((N_DOM, ROWS, D), jnp.float32).at[owners, safe_rows].add(weighted)
    boundary_degree = jnp.zeros((N_DOM, ROWS), jnp.float32).at[owners, safe_rows].add(live_mask.astype(jnp.float32))
    degree = 1.0 + local_degree + boundary_degree
    base = partitions.astype(jnp.float32)
    neighbour_mean = ((base + local_sum + boundary_sum) / degree[..., None]).astype(jnp.bfloat16)
    projected = jnp.dot(neighbour_mean.reshape(-1, D), layer_weight, preferred_element_type=jnp.float32).reshape(base.shape) + layer_bias
    summed = base + jnp.maximum(projected, 0.0)
    scaled = summed * lax.rsqrt(lax.optimization_barrier(jnp.mean(summed * summed, axis=-1, keepdims=True)) + 1e-05)
    return (scaled * layer_gain).astype(jnp.bfloat16).reshape(N_DOM * ROWS, D)

def reference(features, weight, bias, gain, tile_col, tile_adj, send_rows, recv_dst):
    states = []
    for layer_now in range(N_LAYER):
        states.append([])
    for span_now in range(SPANS):
        hidden = features[span_now]
        for layer_now in range(N_LAYER):
            hidden = apply_layer(hidden, tile_col[span_now], tile_adj[span_now], send_rows[span_now], recv_dst[span_now], weight[layer_now], bias[layer_now], gain[layer_now])
            states[layer_now].append(hidden)
    return jnp.stack([jnp.stack(row_list) for row_list in states])
```

```python
import functools

import jax
import jax.numpy as jnp
from jax import lax
from jax.experimental import pallas as pl
from jax.experimental.pallas import tpu as pltpu
from jax.sharding import PartitionSpec as P

VMEM = pltpu.VMEM
PACK_ROWS = 16


def whole(count):
    return [pl.BlockSpec(memory_space=VMEM)] * count


def slot_column(table, slots):
    count = table.shape[0]
    rows = count * slots
    expand = (
        lax.broadcasted_iota(jnp.int32, (rows, count), 0) // slots
        == lax.broadcasted_iota(jnp.int32, (rows, count), 1)
    ).astype(jnp.bfloat16)
    spread = jnp.dot(expand, table.astype(jnp.float32).astype(jnp.bfloat16), preferred_element_type=jnp.float32)
    here = lax.broadcasted_iota(jnp.int32, (rows, slots), 0) % slots == lax.broadcasted_iota(
        jnp.int32, (rows, slots), 1
    )
    return jnp.sum(jnp.where(here, spread, 0.0), axis=1, keepdims=True)


def one_hot_rows(column, width):
    ids = lax.broadcasted_iota(jnp.int32, (column.shape[0], width), 1)
    return (column.astype(jnp.int32) == ids).astype(jnp.float32).astype(jnp.bfloat16)


def first_kernel(span_ref, features_ref, send_ref, hidden_ref, select_ref, outgoing_ref):
    hidden = features_ref[0]
    hidden_ref[...] = hidden
    select = one_hot_rows(slot_column(send_ref[0, 0], send_ref.shape[-1]), hidden.shape[0])
    select_ref[...] = select
    outgoing_ref[...] = jnp.dot(select, hidden, preferred_element_type=jnp.float32).astype(jnp.bfloat16)


def first_gather(span, features, send_rows):
    _, rows, width = features.shape
    peers, slots = send_rows.shape[2:]
    return pl.pallas_call(
        first_kernel,
        grid_spec=pltpu.PrefetchScalarGridSpec(
            num_scalar_prefetch=1,
            grid=(1,),
            in_specs=[
                pl.BlockSpec((1, rows, width), lambda i, s: (s[0], 0, 0)),
                pl.BlockSpec((1, 1, peers, slots), lambda i, s: (s[0], 0, 0, 0)),
            ],
            out_specs=[
                pl.BlockSpec((rows, width), lambda i, s: (0, 0)),
                pl.BlockSpec((peers * slots, rows), lambda i, s: (0, 0)),
                pl.BlockSpec((peers * slots, width), lambda i, s: (0, 0)),
            ],
        ),
        out_shape=[
            jax.ShapeDtypeStruct((rows, width), jnp.bfloat16),
            jax.ShapeDtypeStruct((peers * slots, rows), jnp.bfloat16),
            jax.ShapeDtypeStruct((peers * slots, width), jnp.bfloat16),
        ],
        name="first_gather",
    )(span, features, send_rows)


def tables_kernel(span_ref, col_ref, adj_ref, dest_ref, near_ref, scatter_ref, inverse_ref):
    _, blocks, tiles, side, _ = adj_ref.shape
    span = span_ref[0]
    rows = blocks * side
    scatter = one_hot_rows(slot_column(dest_ref[0, 0], dest_ref.shape[-1]), rows).astype(jnp.float32).T
    scatter_ref[...] = scatter.astype(jnp.bfloat16)
    degree = 1.0 + jnp.sum(scatter, axis=1, keepdims=True)
    for r in range(blocks):
        below = slice(r * side, (r + 1) * side)
        local_degree = jnp.zeros((side, 1), jnp.float32)
        for b in range(blocks):
            total = jnp.zeros((side, side), jnp.int32)
            for k in range(tiles):
                hit = col_ref[(span * blocks + r) * tiles + k] == b
                total += jnp.where(hit, adj_ref[0, r, k], 0)
            dense = total.astype(jnp.float32)
            local_degree += jnp.sum(dense, axis=1, keepdims=True)
            if b == r:
                dense += (
                    lax.broadcasted_iota(jnp.int32, (side, side), 0)
                    == lax.broadcasted_iota(jnp.int32, (side, side), 1)
                ).astype(jnp.float32)
            near_ref[below, b * side : (b + 1) * side] = dense.astype(jnp.bfloat16)
        inverse_ref[below, :] = jnp.broadcast_to(
            1.0 / (degree[below] + local_degree), (side, inverse_ref.shape[1])
        )


def build_tables(span, tile_col, tile_adj, recv_dst):
    _, blocks, tiles, side, _ = tile_adj.shape
    rows = blocks * side
    peers, slots = recv_dst.shape[2:]
    return pl.pallas_call(
        tables_kernel,
        grid_spec=pltpu.PrefetchScalarGridSpec(
            num_scalar_prefetch=2,
            grid=(1,),
            in_specs=[
                pl.BlockSpec((1, blocks, tiles, side, side), lambda i, s, c: (s[0], 0, 0, 0, 0)),
                pl.BlockSpec((1, 1, peers, slots), lambda i, s, c: (s[0], 0, 0, 0)),
            ],
            out_specs=[
                pl.BlockSpec((rows, rows), lambda i, s, c: (0, 0)),
                pl.BlockSpec((rows, peers * slots), lambda i, s, c: (0, 0)),
                pl.BlockSpec((rows, side), lambda i, s, c: (0, 0)),
            ],
        ),
        out_shape=[
            jax.ShapeDtypeStruct((rows, rows), jnp.bfloat16),
            jax.ShapeDtypeStruct((rows, peers * slots), jnp.bfloat16),
            jax.ShapeDtypeStruct((rows, side), jnp.float32),
        ],
        name="build_tables",
    )(span, tile_col.reshape(-1), tile_adj, recv_dst)


def layer_math(hidden_ref, arrived_ref, near_ref, scatter_ref, inverse_ref, pack_ref):
    rows, width = hidden_ref.shape
    hidden = hidden_ref[...]
    total = jnp.dot(near_ref[...], hidden, preferred_element_type=jnp.float32)
    total += jnp.dot(scatter_ref[...], arrived_ref[...], preferred_element_type=jnp.float32)
    inverse = jnp.concatenate([inverse_ref[...]] * (width // inverse_ref.shape[1]), axis=1)
    mean = (total * inverse).astype(jnp.bfloat16)
    vectors = pack_ref[width : width + PACK_ROWS, :].astype(jnp.float32)
    bias = vectors[0:1] + vectors[1:2]
    gain = vectors[2:3] + vectors[3:4]
    projected = jnp.dot(mean, pack_ref[0:width, :], preferred_element_type=jnp.float32) + bias
    summed = hidden.astype(jnp.float32) + jnp.maximum(projected, 0.0)
    scale = lax.rsqrt(jnp.mean(summed * summed, axis=1, keepdims=True) + 1e-05)
    return (summed * scale * gain).astype(jnp.bfloat16)


def layer_kernel(
    hidden_ref, arrived_ref, near_ref, scatter_ref, inverse_ref, pack_ref, select_ref, next_ref, outgoing_ref
):
    state = layer_math(hidden_ref, arrived_ref, near_ref, scatter_ref, inverse_ref, pack_ref)
    next_ref[...] = state
    outgoing_ref[...] = jnp.dot(select_ref[...], state, preferred_element_type=jnp.float32).astype(jnp.bfloat16)


def last_kernel(hidden_ref, arrived_ref, near_ref, scatter_ref, inverse_ref, pack_ref, next_ref):
    next_ref[...] = layer_math(hidden_ref, arrived_ref, near_ref, scatter_ref, inverse_ref, pack_ref)


def run_layer(hidden, arrived, tables, pack, select):
    state = jax.ShapeDtypeStruct(hidden.shape, jnp.bfloat16)
    if select is None:
        return pl.pallas_call(
            last_kernel,
            out_shape=state,
            in_specs=whole(6),
            out_specs=pl.BlockSpec(memory_space=VMEM),
            name="last_layer",
        )(hidden, arrived, *tables, pack), None
    return pl.pallas_call(
        layer_kernel,
        out_shape=[state, jax.ShapeDtypeStruct((select.shape[0], hidden.shape[1]), jnp.bfloat16)],
        in_specs=whole(7),
        out_specs=whole(2),
        name="layer",
    )(hidden, arrived, *tables, pack, select)


def pack_layer(weight, bias, gain):
    rows = []
    for vector in (bias, gain):
        high = lax.reduce_precision(vector, 8, 7)
        rows += [high, vector - high]
    small = jnp.concatenate(rows + [jnp.zeros((PACK_ROWS - 4, weight.shape[1]), jnp.float32)], axis=0)
    return jnp.concatenate([weight, small.astype(jnp.bfloat16)], axis=0)


def local(features, weight, bias, gain, tile_col, tile_adj, send_rows, recv_dst):
    layers = lax.axis_size("layer")
    plane = lax.axis_index("layer")
    first, last = 0, layers - 1
    peers, slots = send_rows.shape[2:]
    width = features.shape[-1]
    span = (2 * plane >= layers).astype(jnp.int32).reshape(1)
    hidden, select, outgoing = first_gather(span, features, send_rows)
    own_pack = pack_layer(weight[0], bias, gain)
    tables = build_tables(span, tile_col, tile_adj, recv_dst)

    previous = before = None
    came = own_pack
    kept = [None, None]
    for step in range(layers):
        arrived = lax.all_to_all(outgoing.reshape(peers, slots, width), "dom", 0, 0, tiled=True)
        if step < last:
            arriving = lax.ppermute(own_pack, "layer", [(step, last), (step + 1, first)])
        else:
            arriving = own_pack
        pack = jnp.where(plane == first, came, arriving)
        came = arriving
        if step >= 2:
            back = lax.ppermute(
                jnp.where(plane == first, hidden, previous), "layer", [(first, step - 1), (last, step - 2)]
            )
            kept[0] = jnp.where(plane == step - 1, back, kept[0])
            kept[1] = back if kept[1] is None else jnp.where(plane == step - 2, back, kept[1])
        previous, before = hidden, previous
        hidden, outgoing = run_layer(
            hidden, arrived.reshape(peers * slots, width), tables, pack, select if step < last else None
        )
        if step == 0:
            kept[0] = hidden
    back = lax.ppermute(
        jnp.where(plane == first, hidden, previous), "layer", [(first, last), (last, last - 1)]
    )
    kept[0] = jnp.where(plane == last, back, kept[0])
    kept[1] = jnp.where(plane == last, hidden, jnp.where(plane == last - 1, back, kept[1]))
    return jnp.stack(kept)[None]


def solution(mesh):
    in_specs = (
        P(None, "dom", None),
        P("layer", None, None),
        P("layer", None),
        P("layer", None),
        P(None, "dom", None),
        P(None, "dom", None, None, None),
        P(None, "dom", None, None),
        P(None, "dom", None, None),
    )
    out_specs = P("layer", None, "dom", None)
    return jax.shard_map(local, mesh=mesh, in_specs=in_specs, out_specs=out_specs, check_vma=False)
```

```python
import functools

import jax
import jax.numpy as jnp
from jax import lax
from jax.experimental import pallas as pl
from jax.experimental.pallas import tpu as pltpu
from jax.sharding import PartitionSpec as P

PACK_ROWS = 16
KERNEL_VMEM = 8 * 2**20
VMEM = pl.BlockSpec(memory_space=pltpu.VMEM)
SMEM = pl.BlockSpec(memory_space=pltpu.SMEM)
ANYWHERE = pl.BlockSpec(memory_space=pl.ANY)
PARAMS = pltpu.CompilerParams(vmem_limit_bytes=KERNEL_VMEM)
WIDE_PARAMS = pltpu.CompilerParams(vmem_limit_bytes=56 * 2**20)
CHUNKS = 4


def slot_column(table):
    slots, count = table.shape
    rows = count * slots
    expand = (
        lax.broadcasted_iota(jnp.int32, (rows, count), 0) // slots
        == lax.broadcasted_iota(jnp.int32, (rows, count), 1)
    ).astype(jnp.bfloat16)
    spread = lax.dot_general(
        expand,
        table.astype(jnp.float32).astype(jnp.bfloat16),
        (((1,), (1,)), ((), ())),
        preferred_element_type=jnp.float32,
    )
    here = lax.broadcasted_iota(jnp.int32, (rows, slots), 0) % slots == lax.broadcasted_iota(
        jnp.int32, (rows, slots), 1
    )
    return jnp.sum(jnp.where(here, spread, 0.0), axis=1, keepdims=True)


def one_hot_rows(column, width):
    ids = lax.broadcasted_iota(jnp.int32, (column.shape[0], width), 1)
    return (column.astype(jnp.int32) == ids).astype(jnp.float32).astype(jnp.bfloat16)


def gather_out(select_ref, state, outgoing_ref, staged_ref, sems):
    size = select_ref.shape[0] // CHUNKS
    copies = []
    for chunk in range(CHUNKS):
        at = pl.ds(chunk * size, size)
        staged_ref[at, :] = jnp.dot(
            select_ref[at, :], state, preferred_element_type=jnp.float32
        ).astype(jnp.bfloat16)
        copies.append(pltpu.make_async_copy(staged_ref.at[at], outgoing_ref.at[at], sems.at[chunk]))
        copies[-1].start()
    for copy in copies:
        copy.wait()


def gather_scratch(slots, width):
    return [pltpu.VMEM((slots, width), jnp.bfloat16), pltpu.SemaphoreType.DMA((CHUNKS,))]


def first_kernel(span_ref, features_ref, send_ref, outgoing_ref, select_ref, staged_ref, sems):
    select_ref[...] = one_hot_rows(slot_column(send_ref[0, 0]), features_ref.shape[1])
    gather_out(select_ref, features_ref[0], outgoing_ref, staged_ref, sems)


def first_gather(span, features, send_rows):
    _, rows, width = features.shape
    slots, peers = send_rows.shape[2:]
    return pl.pallas_call(
        first_kernel,
        grid_spec=pltpu.PrefetchScalarGridSpec(
            num_scalar_prefetch=1,
            grid=(1,),
            in_specs=[
                pl.BlockSpec((1, rows, width), lambda i, s: (s[0], 0, 0)),
                pl.BlockSpec((1, 1, slots, peers), lambda i, s: (s[0], 0, 0, 0)),
            ],
            out_specs=ANYWHERE,
            scratch_shapes=[pltpu.VMEM((peers * slots, rows), jnp.bfloat16)]
            + gather_scratch(peers * slots, width),
        ),
        out_shape=jax.ShapeDtypeStruct((peers * slots, width), jnp.bfloat16),
        compiler_params=WIDE_PARAMS,
        name="first_gather",
    )(span, features, send_rows)


def tables_kernel(
    span_ref,
    col_ref,
    adj_ref,
    dest_ref,
    send_ref,
    features_ref,
    after_ref,
    near_ref,
    scatter_ref,
    inverse_ref,
    select_ref,
    hidden_ref,
):
    hidden_ref[...] = features_ref[0]
    select_ref[...] = one_hot_rows(slot_column(send_ref[0, 0]), hidden_ref.shape[0])
    _, blocks, tiles, side, _ = adj_ref.shape
    span = span_ref[0]
    rows = blocks * side
    scatter = one_hot_rows(slot_column(dest_ref[0, 0]), rows).astype(jnp.float32).T
    scatter_ref[...] = scatter.astype(jnp.bfloat16)
    degree = 1.0 + jnp.sum(scatter, axis=1, keepdims=True)
    for r in range(blocks):
        below = slice(r * side, (r + 1) * side)
        local_degree = jnp.zeros((side, 1), jnp.float32)
        for b in range(blocks):
            total = jnp.zeros((side, side), jnp.int32)
            for k in range(tiles):
                hit = col_ref[span, r, k] == b
                total += jnp.where(hit, adj_ref[0, r, k], 0)
            dense = total.astype(jnp.float32)
            local_degree += jnp.sum(dense, axis=1, keepdims=True)
            if b == r:
                dense += (
                    lax.broadcasted_iota(jnp.int32, (side, side), 0)
                    == lax.broadcasted_iota(jnp.int32, (side, side), 1)
                ).astype(jnp.float32)
            near_ref[below, b * side : (b + 1) * side] = dense.astype(jnp.bfloat16)
        inverse_ref[below, :] = jnp.broadcast_to(
            1.0 / (degree[below] + local_degree), (side, inverse_ref.shape[1])
        )


def build_tables(span, tile_col, tile_adj, recv_dst, send_rows, features, after):
    _, blocks, tiles, side, _ = tile_adj.shape
    _, rows, width = features.shape
    slots, peers = recv_dst.shape[2:]
    shapes = [
        ((rows, rows), jnp.bfloat16),
        ((rows, peers * slots), jnp.bfloat16),
        ((rows, side), jnp.float32),
        ((peers * slots, rows), jnp.bfloat16),
        ((rows, width), jnp.bfloat16),
    ]
    return pl.pallas_call(
        tables_kernel,
        grid_spec=pltpu.PrefetchScalarGridSpec(
            num_scalar_prefetch=1,
            grid=(1,),
            in_specs=[
                SMEM,
                pl.BlockSpec((1, blocks, tiles, side, side), lambda i, s: (s[0], 0, 0, 0, 0)),
                pl.BlockSpec((1, 1, slots, peers), lambda i, s: (s[0], 0, 0, 0)),
                pl.BlockSpec((1, 1, slots, peers), lambda i, s: (s[0], 0, 0, 0)),
                pl.BlockSpec((1, rows, width), lambda i, s: (s[0], 0, 0)),
                ANYWHERE,
            ],
            out_specs=[pl.BlockSpec(shape, lambda i, s: (0, 0)) for shape, _ in shapes],
        ),
        out_shape=[jax.ShapeDtypeStruct(shape, dtype) for shape, dtype in shapes],
        compiler_params=PARAMS,
        name="build_tables",
    )(span, tile_col, tile_adj, recv_dst, send_rows, features, after)


def pack_kernel(weight_ref, bias_ref, gain_ref, after_ref, pack_ref):
    width = weight_ref.shape[-1]
    pack_ref[0:width, :] = weight_ref[0]
    row = lax.broadcasted_iota(jnp.int32, (PACK_ROWS, width), 0)
    small = jnp.zeros((PACK_ROWS, width), jnp.float32)
    for at, ref in ((0, bias_ref), (2, gain_ref)):
        vector = ref[...]
        high = vector.astype(jnp.bfloat16).astype(jnp.float32)
        small = jnp.where(row == at, high, small)
        small = jnp.where(row == at + 1, vector - high, small)
    pack_ref[width : width + PACK_ROWS, :] = small.astype(jnp.bfloat16)


def pack_layer(weight, bias, gain, after):
    width = weight.shape[-1]
    return pl.pallas_call(
        pack_kernel,
        out_shape=jax.ShapeDtypeStruct((width + PACK_ROWS, width), jnp.bfloat16),
        in_specs=[VMEM] * 3 + [ANYWHERE],
        out_specs=VMEM,
        compiler_params=WIDE_PARAMS,
        name="pack_layer",
    )(weight, bias, gain, after)


def layer_kernel(
    step,
    layers,
    plane_ref,
    hidden_ref,
    arrived_ref,
    near_ref,
    scatter_ref,
    inverse_ref,
    select_ref,
    early_ref,
    late_ref,
    after_ref,
    state_ref,
    *refs,
):
    rows, width = hidden_ref.shape
    plane = plane_ref[0]
    begin = jnp.where(plane == 0, 0, layers - 1 - plane)
    pack = jnp.where(plane == 0, early_ref[...], late_ref[...])
    hidden = hidden_ref[...]
    total = jnp.dot(near_ref[...], hidden, preferred_element_type=jnp.float32)
    total += jnp.dot(scatter_ref[...], arrived_ref[...], preferred_element_type=jnp.float32)
    inverse = jnp.concatenate([inverse_ref[...]] * (width // inverse_ref.shape[1]), axis=1)
    mean = (total * inverse).astype(jnp.bfloat16)
    vectors = pack[width : width + PACK_ROWS, :].astype(jnp.float32)
    bias = vectors[0:1] + vectors[1:2]
    gain = vectors[2:3] + vectors[3:4]
    projected = jnp.dot(mean, pack[0:width, :], preferred_element_type=jnp.float32) + bias
    summed = hidden.astype(jnp.float32) + jnp.maximum(projected, 0.0)
    scale = lax.rsqrt(jnp.mean(summed * summed, axis=1, keepdims=True) + 1e-05)
    state = (summed * scale * gain).astype(jnp.bfloat16)
    if step < layers - 1:
        state = jnp.where(step >= begin, state, hidden)
    state_ref[...] = state
    if step < layers - 1:
        carried_ref, outgoing_ref, staged_ref, sems = refs
        carried_ref[...] = late_ref[...]
        gather_out(select_ref, state, outgoing_ref, staged_ref, sems)


def run_layer(step, layers, plane, hidden, arrived, tables, early, late, after):
    slots, width = arrived.shape
    outs = [hidden, late, arrived]
    out_specs = [VMEM, VMEM, ANYWHERE]
    scratch = gather_scratch(slots, width)
    if step == layers - 1:
        outs, out_specs, scratch = outs[:1], out_specs[:1], []
    return pl.pallas_call(
        functools.partial(layer_kernel, step, layers),
        out_shape=[jax.ShapeDtypeStruct(out.shape, jnp.bfloat16) for out in outs],
        in_specs=[SMEM] + [VMEM] * 8 + [ANYWHERE],
        out_specs=out_specs,
        scratch_shapes=scratch,
        compiler_params=PARAMS,
        name="layer",
    )(plane, hidden, arrived, *tables, early, late, after)


def local(features, weight, bias, gain, tile_col, tile_adj, send_rows, recv_dst):
    layers = lax.axis_size("layer")
    index = lax.axis_index("layer")
    peers, slots = send_rows.shape[2:]
    width = features.shape[-1]
    plane = index.reshape(1)
    span = plane % 2
    send_rows = send_rows.transpose(0, 1, 3, 2)
    recv_dst = recv_dst.transpose(0, 1, 3, 2)
    down = [(z, (z - 1) % layers) for z in range(layers)]

    outgoing = first_gather(span, features, send_rows)
    own_pack = pack_layer(weight, bias, gain, outgoing)
    *tables, hidden = build_tables(span, tile_col, tile_adj, recv_dst, send_rows, features, outgoing)
    early = carried = own_pack
    for step in range(layers):
        arrived = lax.all_to_all(outgoing.reshape(peers, slots, width), "dom", 0, 0, tiled=True)
        arrived = arrived.reshape(peers * slots, width)
        if step < layers - 1:
            late = after = lax.ppermute(carried, "layer", down)
        else:
            late = own_pack
            after = from_above = lax.ppermute(hidden, "layer", down[1:])
        hidden, *more = run_layer(step, layers, plane, hidden, arrived, tables, early, late, after)
        if more:
            carried, outgoing = more
            early = carried
        if step == 0:
            first_state = hidden
    last_state = lax.ppermute(hidden, "layer", down[:1])
    own = jnp.where(index == 0, first_state, hidden)
    other = jnp.where(index == layers - 1, last_state, from_above)
    even = index % 2 == 0
    return jnp.stack([jnp.where(even, own, other), jnp.where(even, other, own)])[None]


def solution(mesh):
    in_specs = (
        P(None, "dom", None),
        P("layer", None, None),
        P("layer", None),
        P("layer", None),
        P(None, "dom", None),
        P(None, "dom", None, None, None),
        P(None, "dom", None, None),
        P(None, "dom", None, None),
    )
    out_specs = P("layer", None, "dom", None)
    return jax.shard_map(local, mesh=mesh, in_specs=in_specs, out_specs=out_specs, check_vma=False)
```

```python
import functools

import jax
import jax.numpy as jnp
from jax import lax
from jax.experimental import pallas as pl
from jax.experimental.pallas import tpu as pltpu
from jax.sharding import PartitionSpec as P

PACK_ROWS = 32
KERNEL_VMEM = 8 * 2**20
VMEM = pl.BlockSpec(memory_space=pltpu.VMEM)
SMEM = pl.BlockSpec(memory_space=pltpu.SMEM)
ANYWHERE = pl.BlockSpec(memory_space=pl.ANY)
PARAMS = pltpu.CompilerParams(vmem_limit_bytes=KERNEL_VMEM)
WIDE_PARAMS = pltpu.CompilerParams(vmem_limit_bytes=56 * 2**20)
CHUNKS = 4


def slot_column(table):
    slots, count = table.shape
    rows = count * slots
    expand = (
        lax.broadcasted_iota(jnp.int32, (rows, count), 0) // slots
        == lax.broadcasted_iota(jnp.int32, (rows, count), 1)
    ).astype(jnp.bfloat16)
    spread = lax.dot_general(
        expand,
        table.astype(jnp.float32).astype(jnp.bfloat16),
        (((1,), (1,)), ((), ())),
        preferred_element_type=jnp.float32,
    )
    here = lax.broadcasted_iota(jnp.int32, (rows, slots), 0) % slots == lax.broadcasted_iota(
        jnp.int32, (rows, slots), 1
    )
    return jnp.sum(jnp.where(here, spread, 0.0), axis=1, keepdims=True)


def one_hot_rows(column, width):
    ids = lax.broadcasted_iota(jnp.int32, (column.shape[0], width), 1)
    return (column.astype(jnp.int32) == ids).astype(jnp.float32).astype(jnp.bfloat16)


def gather_out(select_ref, state, outgoing_ref, staged_ref, sems):
    size = select_ref.shape[0] // CHUNKS
    copies = []
    for chunk in range(CHUNKS):
        at = pl.ds(chunk * size, size)
        staged_ref[at, :] = jnp.dot(
            select_ref[at, :], state, preferred_element_type=jnp.float32
        ).astype(jnp.bfloat16)
        copies.append(pltpu.make_async_copy(staged_ref.at[at], outgoing_ref.at[at], sems.at[chunk]))
        copies[-1].start()
    for copy in copies:
        copy.wait()


def gather_scratch(slots, width):
    return [pltpu.VMEM((slots, width), jnp.bfloat16), pltpu.SemaphoreType.DMA((CHUNKS,))]


def pack_rows(weight_ref, bias_ref, gain_ref, pack_ref):
    width = weight_ref.shape[-1]
    pack_ref[0:width, :] = weight_ref[0]
    row = lax.broadcasted_iota(jnp.int32, (PACK_ROWS, width), 0)
    small = jnp.zeros((PACK_ROWS, width), jnp.float32)
    for at, ref in ((0, bias_ref), (2, gain_ref)):
        vector = ref[...]
        high = vector.astype(jnp.bfloat16).astype(jnp.float32)
        small = jnp.where(row == at, high, small)
        small = jnp.where(row == at + 1, vector - high, small)
    pack_ref[width : width + PACK_ROWS, :] = small.astype(jnp.bfloat16)


def first_kernel(
    span_ref,
    core_ref,
    features_ref,
    send_ref,
    weight_ref,
    bias_ref,
    gain_ref,
    outgoing_ref,
    own_ref,
    half_ref,
    select_ref,
    pack_ref,
    part_ref,
    pack_sems,
    staged_ref,
    sems,
):
    pack_rows(weight_ref, bias_ref, gain_ref, pack_ref)
    rows = part_ref.shape[0]
    part_ref[...] = jnp.where(core_ref[0] == 0, pack_ref[0:rows, :], pack_ref[rows : 2 * rows, :])
    copies = [
        pltpu.make_async_copy(part_ref, half_ref, pack_sems.at[0]),
        pltpu.make_async_copy(pack_ref, own_ref, pack_sems.at[1]),
    ]
    for copy in copies:
        copy.start()
    select_ref[...] = one_hot_rows(slot_column(send_ref[0, 0]), features_ref.shape[1])
    gather_out(select_ref, features_ref[0], outgoing_ref, staged_ref, sems)
    for copy in copies:
        copy.wait()


def first_gather(span, core, features, send_rows, weight, bias, gain):
    _, rows, width = features.shape
    slots, peers = send_rows.shape[2:]
    pack = (width + PACK_ROWS, width)
    half = (pack[0] // 2, width)
    return pl.pallas_call(
        first_kernel,
        grid_spec=pltpu.PrefetchScalarGridSpec(
            num_scalar_prefetch=2,
            grid=(1,),
            in_specs=[
                pl.BlockSpec((1, rows, width), lambda i, s, c: (s[0], 0, 0)),
                pl.BlockSpec((1, 1, slots, peers), lambda i, s, c: (s[0], 0, 0, 0)),
                pl.BlockSpec(weight.shape, lambda i, s, c: (0, 0, 0)),
                pl.BlockSpec(bias.shape, lambda i, s, c: (0, 0)),
                pl.BlockSpec(gain.shape, lambda i, s, c: (0, 0)),
            ],
            out_specs=[ANYWHERE] * 3,
            scratch_shapes=[
                pltpu.VMEM((peers * slots, rows), jnp.bfloat16),
                pltpu.VMEM(pack, jnp.bfloat16),
                pltpu.VMEM(half, jnp.bfloat16),
                pltpu.SemaphoreType.DMA((2,)),
            ]
            + gather_scratch(peers * slots, width),
        ),
        out_shape=[
            jax.ShapeDtypeStruct(shape, jnp.bfloat16) for shape in ((peers * slots, width), pack, half)
        ],
        compiler_params=WIDE_PARAMS,
        name="first_gather",
    )(span, core, features, send_rows, weight, bias, gain)


def tables_kernel(
    span_ref,
    col_ref,
    adj_ref,
    dest_ref,
    send_ref,
    features_ref,
    after_ref,
    near_ref,
    scatter_ref,
    inverse_ref,
    select_ref,
    hidden_ref,
):
    hidden_ref[...] = features_ref[0]
    select_ref[...] = one_hot_rows(slot_column(send_ref[0, 0]), hidden_ref.shape[0])
    _, blocks, tiles, side, _ = adj_ref.shape
    span = span_ref[0]
    rows = blocks * side
    scatter = one_hot_rows(slot_column(dest_ref[0, 0]), rows).astype(jnp.float32).T
    scatter_ref[...] = scatter.astype(jnp.bfloat16)
    degree = 1.0 + jnp.sum(scatter, axis=1, keepdims=True)
    for r in range(blocks):
        below = slice(r * side, (r + 1) * side)
        local_degree = jnp.zeros((side, 1), jnp.float32)
        for b in range(blocks):
            total = jnp.zeros((side, side), jnp.int32)
            for k in range(tiles):
                hit = col_ref[span, r, k] == b
                total += jnp.where(hit, adj_ref[0, r, k], 0)
            dense = total.astype(jnp.float32)
            local_degree += jnp.sum(dense, axis=1, keepdims=True)
            if b == r:
                dense += (
                    lax.broadcasted_iota(jnp.int32, (side, side), 0)
                    == lax.broadcasted_iota(jnp.int32, (side, side), 1)
                ).astype(jnp.float32)
            near_ref[below, b * side : (b + 1) * side] = dense.astype(jnp.bfloat16)
        inverse_ref[below, :] = jnp.broadcast_to(
            1.0 / (degree[below] + local_degree), (side, inverse_ref.shape[1])
        )


def build_tables(span, tile_col, tile_adj, recv_dst, send_rows, features, after):
    _, blocks, tiles, side, _ = tile_adj.shape
    _, rows, width = features.shape
    slots, peers = recv_dst.shape[2:]
    shapes = [
        ((rows, rows), jnp.bfloat16),
        ((rows, peers * slots), jnp.bfloat16),
        ((rows, side), jnp.float32),
        ((peers * slots, rows), jnp.bfloat16),
        ((rows, width), jnp.bfloat16),
    ]
    return pl.pallas_call(
        tables_kernel,
        grid_spec=pltpu.PrefetchScalarGridSpec(
            num_scalar_prefetch=1,
            grid=(1,),
            in_specs=[
                SMEM,
                pl.BlockSpec((1, blocks, tiles, side, side), lambda i, s: (s[0], 0, 0, 0, 0)),
                pl.BlockSpec((1, 1, slots, peers), lambda i, s: (s[0], 0, 0, 0)),
                pl.BlockSpec((1, 1, slots, peers), lambda i, s: (s[0], 0, 0, 0)),
                pl.BlockSpec((1, rows, width), lambda i, s: (s[0], 0, 0)),
                ANYWHERE,
            ],
            out_specs=[pl.BlockSpec(shape, lambda i, s: (0, 0)) for shape, _ in shapes],
        ),
        out_shape=[jax.ShapeDtypeStruct(shape, dtype) for shape, dtype in shapes],
        compiler_params=PARAMS,
        name="build_tables",
    )(span, tile_col, tile_adj, recv_dst, send_rows, features, after)


def layer_kernel(
    step,
    layers,
    passed,
    plane_ref,
    hidden_ref,
    arrived_ref,
    near_ref,
    scatter_ref,
    inverse_ref,
    select_ref,
    early_ref,
    late_ref,
    *refs,
):
    passed_in, refs = refs[:passed], refs[passed:]
    rows, width = hidden_ref.shape
    plane = plane_ref[0]
    begin = jnp.where(plane == 0, 0, layers - 1 - plane)
    pack = jnp.where(plane == 0, early_ref[...], late_ref[...])
    hidden = hidden_ref[...]
    total = jnp.dot(near_ref[...], hidden, preferred_element_type=jnp.float32)
    total += jnp.dot(scatter_ref[...], arrived_ref[...], preferred_element_type=jnp.float32)
    inverse = jnp.concatenate([inverse_ref[...]] * (width // inverse_ref.shape[1]), axis=1)
    mean = (total * inverse).astype(jnp.bfloat16)
    vectors = pack[width : width + PACK_ROWS, :].astype(jnp.float32)
    bias = vectors[0:1] + vectors[1:2]
    gain = vectors[2:3] + vectors[3:4]
    projected = jnp.dot(mean, pack[0:width, :], preferred_element_type=jnp.float32) + bias
    summed = hidden.astype(jnp.float32) + jnp.maximum(projected, 0.0)
    scale = lax.rsqrt(jnp.mean(summed * summed, axis=1, keepdims=True) + 1e-05)
    state = (summed * scale * gain).astype(jnp.bfloat16)
    if step == layers - 1:
        own_ref, send_ref = refs
        own_ref[...] = jnp.where(plane == 0, passed_in[0][...], state)
        send_ref[...] = jnp.where(plane == 0, state, hidden)
        return
    state = jnp.where(step >= begin, state, hidden)
    state_ref, outgoing_ref, *refs = refs
    state_ref[...] = state
    outgoing_ref[...] = jnp.dot(select_ref[...], state, preferred_element_type=jnp.float32).astype(jnp.bfloat16)
    for source_ref, target_ref in zip(passed_in, refs):
        target_ref[...] = source_ref[...]


def run_layer(step, layers, plane, hidden, arrived, tables, early, late, passed=()):
    outs = [jax.ShapeDtypeStruct(hidden.shape, jnp.bfloat16)]
    if step == layers - 1:
        outs *= 2
    else:
        outs.append(pltpu.VMEM(arrived.shape, jnp.bfloat16))
        outs += [jax.ShapeDtypeStruct(array.shape, jnp.bfloat16) for array in passed]
    return pl.pallas_call(
        functools.partial(layer_kernel, step, layers, len(passed)),
        out_shape=outs,
        in_specs=[SMEM] + [VMEM] * (8 + len(passed)),
        out_specs=[VMEM] * len(outs),
        compiler_params=PARAMS,
        name="layer",
    )(plane, hidden, arrived, *tables, early, late, *passed)


def local(features, weight, bias, gain, tile_col, tile_adj, send_rows, recv_dst):
    layers = lax.axis_size("layer")
    index = lax.axis_index("layer")
    peers, slots = send_rows.shape[2:]
    width = features.shape[-1]
    plane = index.reshape(1)
    core = (lax.axis_index("dom") % 2).reshape(1)
    span = (index % 2).reshape(1)
    cores = [[2 * chip, 2 * chip + 1] for chip in range(peers // 2)]
    down = [(z, (z - 1) % layers) for z in range(layers)]
    two_down = [(z, (z - 2) % layers) for z in range(layers)]
    send_rows = send_rows.transpose(0, 1, 3, 2)
    recv_dst = recv_dst.transpose(0, 1, 3, 2)

    outgoing, own_pack, own_half = first_gather(span, core, features, send_rows, weight, bias, gain)
    *tables, hidden = build_tables(span, tile_col, tile_adj, recv_dst, send_rows, features, outgoing)
    early = own_pack
    for step in range(layers - 1):
        arrived = lax.all_to_all(outgoing.reshape(peers, slots, width), "dom", 0, 0, tiled=True)
        arrived = arrived.reshape(peers * slots, width)
        if step == 0:
            half = lax.ppermute(own_half, "layer", down)
        late = lax.all_gather(half, "dom", axis_index_groups=cores, tiled=True)
        passed = []
        if step < layers - 2:
            source, pairs = (own_half, two_down) if step == 0 else (half, down)
            passed = [lax.ppermute(source, "layer", pairs)]
        hidden, outgoing, *more = run_layer(
            step, layers, plane, hidden, arrived, tables, early, late, passed
        )
        if more:
            half = more[0]
        if step == 0:
            first_state = hidden
        early = late
    arrived = lax.all_to_all(outgoing.reshape(peers, slots, width), "dom", 0, 0, tiled=True)
    arrived = arrived.reshape(peers * slots, width)
    own, send = run_layer(layers - 1, layers, plane, hidden, arrived, tables, early, own_pack, [first_state])
    swapped = lax.ppermute(send, "layer", down)
    even = index % 2 == 0
    return jnp.stack([jnp.where(even, own, swapped), jnp.where(even, swapped, own)])[None]


def solution(mesh):
    in_specs = (
        P(None, "dom", None),
        P("layer", None, None),
        P("layer", None),
        P("layer", None),
        P(None, "dom", None),
        P(None, "dom", None, None, None),
        P(None, "dom", None, None),
        P(None, "dom", None, None),
    )
    out_specs = P("layer", None, "dom", None)
    return jax.shard_map(local, mesh=mesh, in_specs=in_specs, out_specs=out_specs, check_vma=False)
```

```python
import functools

import jax
import jax.numpy as jnp
from jax import lax
from jax.experimental import pallas as pl
from jax.experimental.pallas import tpu as pltpu
from jax.sharding import PartitionSpec as P

PACK_ROWS = 32
KERNEL_VMEM = 8 * 2**20
VMEM = pl.BlockSpec(memory_space=pltpu.VMEM)
SMEM = pl.BlockSpec(memory_space=pltpu.SMEM)
ANYWHERE = pl.BlockSpec(memory_space=pl.ANY)
PARAMS = pltpu.CompilerParams(vmem_limit_bytes=KERNEL_VMEM)
WIDE_PARAMS = pltpu.CompilerParams(vmem_limit_bytes=56 * 2**20)
CHUNKS = 4


def slot_column(table):
    slots, count = table.shape
    rows = count * slots
    expand = (
        lax.broadcasted_iota(jnp.int32, (rows, count), 0) // slots
        == lax.broadcasted_iota(jnp.int32, (rows, count), 1)
    ).astype(jnp.bfloat16)
    spread = lax.dot_general(
        expand,
        table.astype(jnp.float32).astype(jnp.bfloat16),
        (((1,), (1,)), ((), ())),
        preferred_element_type=jnp.float32,
    )
    here = lax.broadcasted_iota(jnp.int32, (rows, slots), 0) % slots == lax.broadcasted_iota(
        jnp.int32, (rows, slots), 1
    )
    return jnp.sum(jnp.where(here, spread, 0.0), axis=1, keepdims=True)


def one_hot_rows(column, width):
    ids = lax.broadcasted_iota(jnp.int32, (column.shape[0], width), 1)
    return (column.astype(jnp.int32) == ids).astype(jnp.float32).astype(jnp.bfloat16)


def gather_out(select_ref, state, outgoing_ref, staged_ref, sems):
    size = select_ref.shape[0] // CHUNKS
    copies = []
    for chunk in range(CHUNKS):
        at = pl.ds(chunk * size, size)
        staged_ref[at, :] = jnp.dot(
            select_ref[at, :], state, preferred_element_type=jnp.float32
        ).astype(jnp.bfloat16)
        copies.append(pltpu.make_async_copy(staged_ref.at[at], outgoing_ref.at[at], sems.at[chunk]))
        copies[-1].start()
    for copy in copies:
        copy.wait()


def gather_scratch(slots, width):
    return [pltpu.VMEM((slots, width), jnp.bfloat16), pltpu.SemaphoreType.DMA((CHUNKS,))]


def pack_rows(weight_ref, bias_ref, gain_ref, pack_ref):
    width = weight_ref.shape[-1]
    pack_ref[0:width, :] = weight_ref[0]
    row = lax.broadcasted_iota(jnp.int32, (PACK_ROWS, width), 0)
    small = jnp.zeros((PACK_ROWS, width), jnp.float32)
    for at, ref in ((0, bias_ref), (2, gain_ref)):
        vector = ref[...]
        high = vector.astype(jnp.bfloat16).astype(jnp.float32)
        small = jnp.where(row == at, high, small)
        small = jnp.where(row == at + 1, vector - high, small)
    pack_ref[width : width + PACK_ROWS, :] = small.astype(jnp.bfloat16)


def first_kernel(
    span_ref,
    core_ref,
    features_ref,
    send_ref,
    weight_ref,
    bias_ref,
    gain_ref,
    outgoing_ref,
    own_ref,
    half_ref,
    select_ref,
    pack_ref,
    part_ref,
    pack_sems,
    staged_ref,
    sems,
):
    pack_rows(weight_ref, bias_ref, gain_ref, pack_ref)
    rows = part_ref.shape[0]
    part_ref[...] = jnp.where(core_ref[0] == 0, pack_ref[0:rows, :], pack_ref[rows : 2 * rows, :])
    copies = [
        pltpu.make_async_copy(part_ref, half_ref, pack_sems.at[0]),
        pltpu.make_async_copy(pack_ref, own_ref, pack_sems.at[1]),
    ]
    for copy in copies:
        copy.start()
    select_ref[...] = one_hot_rows(slot_column(send_ref[0, 0]), features_ref.shape[1])
    gather_out(select_ref, features_ref[0], outgoing_ref, staged_ref, sems)
    for copy in copies:
        copy.wait()


def first_gather(span, core, features, send_rows, weight, bias, gain):
    _, rows, width = features.shape
    slots, peers = send_rows.shape[2:]
    pack = (width + PACK_ROWS, width)
    half = (pack[0] // 2, width)
    return pl.pallas_call(
        first_kernel,
        grid_spec=pltpu.PrefetchScalarGridSpec(
            num_scalar_prefetch=2,
            grid=(1,),
            in_specs=[
                pl.BlockSpec((1, rows, width), lambda i, s, c: (s[0], 0, 0)),
                pl.BlockSpec((1, 1, slots, peers), lambda i, s, c: (s[0], 0, 0, 0)),
                pl.BlockSpec(weight.shape, lambda i, s, c: (0, 0, 0)),
                pl.BlockSpec(bias.shape, lambda i, s, c: (0, 0)),
                pl.BlockSpec(gain.shape, lambda i, s, c: (0, 0)),
            ],
            out_specs=[ANYWHERE] * 3,
            scratch_shapes=[
                pltpu.VMEM((peers * slots, rows), jnp.bfloat16),
                pltpu.VMEM(pack, jnp.bfloat16),
                pltpu.VMEM(half, jnp.bfloat16),
                pltpu.SemaphoreType.DMA((2,)),
            ]
            + gather_scratch(peers * slots, width),
        ),
        out_shape=[
            jax.ShapeDtypeStruct(shape, jnp.bfloat16) for shape in ((peers * slots, width), pack, half)
        ],
        compiler_params=WIDE_PARAMS,
        name="first_gather",
    )(span, core, features, send_rows, weight, bias, gain)


def tables_kernel(
    span_ref,
    col_ref,
    adj_ref,
    dest_ref,
    send_ref,
    features_ref,
    after_ref,
    near_ref,
    scatter_ref,
    inverse_ref,
    select_ref,
    hidden_ref,
):
    hidden_ref[...] = features_ref[0]
    select_ref[...] = one_hot_rows(slot_column(send_ref[0, 0]), hidden_ref.shape[0])
    _, blocks, tiles, side, _ = adj_ref.shape
    span = span_ref[0]
    rows = blocks * side
    scatter = one_hot_rows(slot_column(dest_ref[0, 0]), rows).astype(jnp.float32).T
    scatter_ref[...] = scatter.astype(jnp.bfloat16)
    degree = 1.0 + jnp.sum(scatter, axis=1, keepdims=True)
    for r in range(blocks):
        below = slice(r * side, (r + 1) * side)
        local_degree = jnp.zeros((side, 1), jnp.float32)
        for b in range(blocks):
            total = jnp.zeros((side, side), jnp.int32)
            for k in range(tiles):
                hit = col_ref[span, r, k] == b
                total += jnp.where(hit, adj_ref[0, r, k], 0)
            dense = total.astype(jnp.float32)
            local_degree += jnp.sum(dense, axis=1, keepdims=True)
            if b == r:
                dense += (
                    lax.broadcasted_iota(jnp.int32, (side, side), 0)
                    == lax.broadcasted_iota(jnp.int32, (side, side), 1)
                ).astype(jnp.float32)
            near_ref[below, b * side : (b + 1) * side] = dense.astype(jnp.bfloat16)
        inverse_ref[below, :] = jnp.broadcast_to(
            1.0 / (degree[below] + local_degree), (side, inverse_ref.shape[1])
        )


def build_tables(span, tile_col, tile_adj, recv_dst, send_rows, features, after):
    _, blocks, tiles, side, _ = tile_adj.shape
    _, rows, width = features.shape
    slots, peers = recv_dst.shape[2:]
    shapes = [
        ((rows, rows), jnp.bfloat16),
        ((rows, peers * slots), jnp.bfloat16),
        ((rows, side), jnp.float32),
        ((peers * slots, rows), jnp.bfloat16),
        ((rows, width), jnp.bfloat16),
    ]
    return pl.pallas_call(
        tables_kernel,
        grid_spec=pltpu.PrefetchScalarGridSpec(
            num_scalar_prefetch=1,
            grid=(1,),
            in_specs=[
                SMEM,
                pl.BlockSpec((1, blocks, tiles, side, side), lambda i, s: (s[0], 0, 0, 0, 0)),
                pl.BlockSpec((1, 1, slots, peers), lambda i, s: (s[0], 0, 0, 0)),
                pl.BlockSpec((1, 1, slots, peers), lambda i, s: (s[0], 0, 0, 0)),
                pl.BlockSpec((1, rows, width), lambda i, s: (s[0], 0, 0)),
                ANYWHERE,
            ],
            out_specs=[pl.BlockSpec(shape, lambda i, s: (0, 0)) for shape, _ in shapes],
        ),
        out_shape=[jax.ShapeDtypeStruct(shape, dtype) for shape, dtype in shapes],
        compiler_params=PARAMS,
        name="build_tables",
    )(span, tile_col, tile_adj, recv_dst, send_rows, features, after)


def layer_kernel(
    step,
    layers,
    passed,
    plane_ref,
    hidden_ref,
    arrived_ref,
    near_ref,
    scatter_ref,
    inverse_ref,
    select_ref,
    early_ref,
    late_ref,
    *refs,
):
    passed_in, refs = refs[:passed], refs[passed:]
    rows, width = hidden_ref.shape
    plane = plane_ref[0]
    begin = jnp.where(plane == 0, 0, layers - 1 - plane)
    pack = jnp.where(plane == 0, early_ref[...], late_ref[...])
    hidden = hidden_ref[...]
    total = jnp.dot(near_ref[...], hidden, preferred_element_type=jnp.float32)
    total += jnp.dot(scatter_ref[...], arrived_ref[...], preferred_element_type=jnp.float32)
    inverse = jnp.concatenate([inverse_ref[...]] * (width // inverse_ref.shape[1]), axis=1)
    mean = (total * inverse).astype(jnp.bfloat16)
    vectors = pack[width : width + PACK_ROWS, :].astype(jnp.float32)
    bias = vectors[0:1] + vectors[1:2]
    gain = vectors[2:3] + vectors[3:4]
    projected = jnp.dot(mean, pack[0:width, :], preferred_element_type=jnp.float32) + bias
    summed = hidden.astype(jnp.float32) + jnp.maximum(projected, 0.0)
    scale = lax.rsqrt(jnp.mean(summed * summed, axis=1, keepdims=True) + 1e-05)
    state = (summed * scale * gain).astype(jnp.bfloat16)
    state_ref, *refs = refs
    if step == layers - 1:
        state_ref[...] = state
        return
    outgoing_ref, *refs = refs
    state = jnp.where(step >= begin, state, hidden)
    state_ref[...] = state
    outgoing_ref[...] = jnp.dot(select_ref[...], state, preferred_element_type=jnp.float32).astype(jnp.bfloat16)
    for source_ref, target_ref in zip(passed_in, refs):
        target_ref[...] = source_ref[...]


def run_layer(step, layers, plane, hidden, arrived, tables, early, late, passed=()):
    outs = [jax.ShapeDtypeStruct(hidden.shape, jnp.bfloat16)]
    if step < layers - 1:
        outs.append(pltpu.VMEM(arrived.shape, jnp.bfloat16))
        outs += [jax.ShapeDtypeStruct(array.shape, jnp.bfloat16) for array in passed]
    return pl.pallas_call(
        functools.partial(layer_kernel, step, layers, len(passed)),
        out_shape=outs,
        in_specs=[SMEM] + [VMEM] * (8 + len(passed)),
        out_specs=[VMEM] * len(outs),
        compiler_params=PARAMS,
        name="layer",
    )(plane, hidden, arrived, *tables, early, late, *passed)


def local(features, weight, bias, gain, tile_col, tile_adj, send_rows, recv_dst):
    layers = lax.axis_size("layer")
    index = lax.axis_index("layer")
    peers, slots = send_rows.shape[2:]
    width = features.shape[-1]
    plane = index.reshape(1)
    core = (lax.axis_index("dom") % 2).reshape(1)
    span = (index % 2).reshape(1)
    cores = [[2 * chip, 2 * chip + 1] for chip in range(peers // 2)]
    down = [(z, (z - 1) % layers) for z in range(layers)]
    two_down = [(z, (z - 2) % layers) for z in range(layers)]
    send_rows = send_rows.transpose(0, 1, 3, 2)
    recv_dst = recv_dst.transpose(0, 1, 3, 2)

    outgoing, own_pack, own_half = first_gather(span, core, features, send_rows, weight, bias, gain)
    *tables, hidden = build_tables(span, tile_col, tile_adj, recv_dst, send_rows, features, outgoing)
    early = own_pack
    for step in range(layers - 1):
        arrived = lax.all_to_all(outgoing.reshape(peers, slots, width), "dom", 0, 0, tiled=True)
        arrived = arrived.reshape(peers * slots, width)
        if step == 0:
            half = lax.ppermute(own_half, "layer", down)
        late = lax.all_gather(half, "dom", axis_index_groups=cores, tiled=True)
        passed = []
        if step < layers - 2:
            source, pairs = (own_half, two_down) if step == 0 else (half, down)
            passed = [lax.ppermute(source, "layer", pairs)]
        hidden, outgoing, *more = run_layer(
            step, layers, plane, hidden, arrived, tables, early, late, passed
        )
        if more:
            half = more[0]
        if step == 0:
            first_state = hidden
        early = late
    last = layers - 1
    from_above = lax.ppermute(hidden, "layer", down[1:])

    def finish(outgoing, hidden):
        arrived = lax.all_to_all(outgoing.reshape(peers, slots, width), "dom", 0, 0, tiled=True)
        arrived = arrived.reshape(peers * slots, width)
        return run_layer(last, layers, plane, hidden, arrived, tables, early, own_pack)[0]

    def idle(outgoing, hidden):
        return jnp.zeros_like(hidden)

    state = lax.cond(index < last, finish, idle, outgoing, hidden)
    full = lax.ppermute(jnp.where(index == 0, state, from_above), "layer", down[:1])
    last_state = lax.cond(index == last, finish, idle, outgoing, hidden)
    own = jnp.where(index == 0, first_state, jnp.where(index == last, last_state, state))
    other = jnp.where(index == last, full, from_above)
    even = index % 2 == 0
    return jnp.stack([jnp.where(even, own, other), jnp.where(even, other, own)])[None]


def solution(mesh):
    in_specs = (
        P(None, "dom", None),
        P("layer", None, None),
        P("layer", None),
        P("layer", None),
        P(None, "dom", None),
        P(None, "dom", None, None, None),
        P(None, "dom", None, None),
        P(None, "dom", None, None),
    )
    out_specs = P("layer", None, "dom", None)
    return jax.shard_map(local, mesh=mesh, in_specs=in_specs, out_specs=out_specs, check_vma=False)
```

```python
import functools

import jax
import jax.numpy as jnp
from jax import lax
from jax.experimental import pallas as pl
from jax.experimental.pallas import tpu as pltpu
from jax.sharding import PartitionSpec as P

PACK_ROWS = 32
KERNEL_VMEM = 8 * 2**20
VMEM = pl.BlockSpec(memory_space=pltpu.VMEM)
SMEM = pl.BlockSpec(memory_space=pltpu.SMEM)
ANYWHERE = pl.BlockSpec(memory_space=pl.ANY)
PARAMS = pltpu.CompilerParams(vmem_limit_bytes=KERNEL_VMEM)
WIDE_PARAMS = pltpu.CompilerParams(vmem_limit_bytes=56 * 2**20)
CHUNKS = 4
FIRST = 40


def slot_column(table):
    slots, count = table.shape
    rows = count * slots
    expand = (
        lax.broadcasted_iota(jnp.int32, (rows, count), 0) // slots
        == (lax.broadcasted_iota(jnp.int32, (rows, count), 1) ^ FIRST)
    ).astype(jnp.bfloat16)
    spread = lax.dot_general(
        expand,
        table.astype(jnp.float32).astype(jnp.bfloat16),
        (((1,), (1,)), ((), ())),
        preferred_element_type=jnp.float32,
    )
    here = lax.broadcasted_iota(jnp.int32, (rows, slots), 0) % slots == lax.broadcasted_iota(
        jnp.int32, (rows, slots), 1
    )
    return jnp.sum(jnp.where(here, spread, 0.0), axis=1, keepdims=True)


def one_hot_rows(column, width):
    ids = lax.broadcasted_iota(jnp.int32, (column.shape[0], width), 1)
    return (column.astype(jnp.int32) == ids).astype(jnp.float32).astype(jnp.bfloat16)


def gather_out(select_ref, state, outgoing_ref, staged_ref, sems):
    size = select_ref.shape[0] // CHUNKS
    copies = []
    for chunk in range(CHUNKS):
        at = pl.ds(chunk * size, size)
        staged_ref[at, :] = jnp.dot(
            select_ref[at, :], state, preferred_element_type=jnp.float32
        ).astype(jnp.bfloat16)
        copies.append(pltpu.make_async_copy(staged_ref.at[at], outgoing_ref.at[at], sems.at[chunk]))
        copies[-1].start()
    for copy in copies:
        copy.wait()


def gather_scratch(slots, width):
    return [pltpu.VMEM((slots, width), jnp.bfloat16), pltpu.SemaphoreType.DMA((CHUNKS,))]


def pack_rows(weight_ref, bias_ref, gain_ref, pack_ref):
    width = weight_ref.shape[-1]
    pack_ref[0:width, :] = weight_ref[0]
    row = lax.broadcasted_iota(jnp.int32, (PACK_ROWS, width), 0)
    small = jnp.zeros((PACK_ROWS, width), jnp.float32)
    for at, ref in ((0, bias_ref), (2, gain_ref)):
        vector = ref[...]
        high = vector.astype(jnp.bfloat16).astype(jnp.float32)
        small = jnp.where(row == at, high, small)
        small = jnp.where(row == at + 1, vector - high, small)
    pack_ref[width : width + PACK_ROWS, :] = small.astype(jnp.bfloat16)


def first_kernel(
    span_ref,
    core_ref,
    features_ref,
    send_ref,
    weight_ref,
    bias_ref,
    gain_ref,
    outgoing_ref,
    own_ref,
    half_ref,
    select_ref,
    pack_ref,
    part_ref,
    pack_sems,
    staged_ref,
    sems,
):
    pack_rows(weight_ref, bias_ref, gain_ref, pack_ref)
    rows = part_ref.shape[0]
    part_ref[...] = jnp.where(core_ref[0] == 0, pack_ref[0:rows, :], pack_ref[rows : 2 * rows, :])
    copies = [
        pltpu.make_async_copy(part_ref, half_ref, pack_sems.at[0]),
        pltpu.make_async_copy(pack_ref, own_ref, pack_sems.at[1]),
    ]
    for copy in copies:
        copy.start()
    select_ref[...] = one_hot_rows(slot_column(send_ref[0, 0]), features_ref.shape[1])
    gather_out(select_ref, features_ref[0], outgoing_ref, staged_ref, sems)
    for copy in copies:
        copy.wait()


def first_gather(span, core, features, send_rows, weight, bias, gain):
    _, rows, width = features.shape
    slots, peers = send_rows.shape[2:]
    pack = (width + PACK_ROWS, width)
    half = (pack[0] // 2, width)
    return pl.pallas_call(
        first_kernel,
        grid_spec=pltpu.PrefetchScalarGridSpec(
            num_scalar_prefetch=2,
            grid=(1,),
            in_specs=[
                pl.BlockSpec((1, rows, width), lambda i, s, c: (s[0], 0, 0)),
                pl.BlockSpec((1, 1, slots, peers), lambda i, s, c: (s[0], 0, 0, 0)),
                pl.BlockSpec(weight.shape, lambda i, s, c: (0, 0, 0)),
                pl.BlockSpec(bias.shape, lambda i, s, c: (0, 0)),
                pl.BlockSpec(gain.shape, lambda i, s, c: (0, 0)),
            ],
            out_specs=[ANYWHERE] * 3,
            scratch_shapes=[
                pltpu.VMEM((peers * slots, rows), jnp.bfloat16),
                pltpu.VMEM(pack, jnp.bfloat16),
                pltpu.VMEM(half, jnp.bfloat16),
                pltpu.SemaphoreType.DMA((2,)),
            ]
            + gather_scratch(peers * slots, width),
        ),
        out_shape=[
            jax.ShapeDtypeStruct(shape, jnp.bfloat16) for shape in ((peers * slots, width), pack, half)
        ],
        compiler_params=WIDE_PARAMS,
        name="first_gather",
    )(span, core, features, send_rows, weight, bias, gain)


def tables_kernel(
    span_ref,
    col_ref,
    adj_ref,
    dest_ref,
    send_ref,
    features_ref,
    after_ref,
    near_ref,
    scatter_ref,
    inverse_ref,
    select_ref,
    hidden_ref,
):
    hidden_ref[...] = features_ref[0]
    select_ref[...] = one_hot_rows(slot_column(send_ref[0, 0]), hidden_ref.shape[0])
    _, blocks, tiles, side, _ = adj_ref.shape
    span = span_ref[0]
    rows = blocks * side
    scatter = one_hot_rows(slot_column(dest_ref[0, 0]), rows).astype(jnp.float32).T
    scatter_ref[...] = scatter.astype(jnp.bfloat16)
    degree = 1.0 + jnp.sum(scatter, axis=1, keepdims=True)
    for r in range(blocks):
        below = slice(r * side, (r + 1) * side)
        local_degree = jnp.zeros((side, 1), jnp.float32)
        for b in range(blocks):
            total = jnp.zeros((side, side), jnp.int32)
            for k in range(tiles):
                hit = col_ref[span, r, k] == b
                total += jnp.where(hit, adj_ref[0, r, k], 0)
            dense = total.astype(jnp.float32)
            local_degree += jnp.sum(dense, axis=1, keepdims=True)
            if b == r:
                dense += (
                    lax.broadcasted_iota(jnp.int32, (side, side), 0)
                    == lax.broadcasted_iota(jnp.int32, (side, side), 1)
                ).astype(jnp.float32)
            near_ref[below, b * side : (b + 1) * side] = dense.astype(jnp.bfloat16)
        inverse_ref[below, :] = jnp.broadcast_to(
            1.0 / (degree[below] + local_degree), (side, inverse_ref.shape[1])
        )


def build_tables(span, tile_col, tile_adj, recv_dst, send_rows, features, after):
    _, blocks, tiles, side, _ = tile_adj.shape
    _, rows, width = features.shape
    slots, peers = recv_dst.shape[2:]
    shapes = [
        ((rows, rows), jnp.bfloat16),
        ((rows, peers * slots), jnp.bfloat16),
        ((rows, side), jnp.float32),
        ((peers * slots, rows), jnp.bfloat16),
        ((rows, width), jnp.bfloat16),
    ]
    return pl.pallas_call(
        tables_kernel,
        grid_spec=pltpu.PrefetchScalarGridSpec(
            num_scalar_prefetch=1,
            grid=(1,),
            in_specs=[
                SMEM,
                pl.BlockSpec((1, blocks, tiles, side, side), lambda i, s: (s[0], 0, 0, 0, 0)),
                pl.BlockSpec((1, 1, slots, peers), lambda i, s: (s[0], 0, 0, 0)),
                pl.BlockSpec((1, 1, slots, peers), lambda i, s: (s[0], 0, 0, 0)),
                pl.BlockSpec((1, rows, width), lambda i, s: (s[0], 0, 0)),
                ANYWHERE,
            ],
            out_specs=[pl.BlockSpec(shape, lambda i, s: (0, 0)) for shape, _ in shapes],
        ),
        out_shape=[jax.ShapeDtypeStruct(shape, dtype) for shape, dtype in shapes],
        compiler_params=PARAMS,
        name="build_tables",
    )(span, tile_col, tile_adj, recv_dst, send_rows, features, after)


def layer_kernel(
    step,
    layers,
    passed,
    plane_ref,
    hidden_ref,
    arrived_ref,
    near_ref,
    scatter_ref,
    inverse_ref,
    select_ref,
    early_ref,
    late_ref,
    *refs,
):
    passed_in, refs = refs[:passed], refs[passed:]
    rows, width = hidden_ref.shape
    plane = plane_ref[0]
    begin = jnp.where(plane == 0, 0, layers - 1 - plane)
    pack = jnp.where(plane == 0, early_ref[...], late_ref[...])
    hidden = hidden_ref[...]
    total = jnp.dot(near_ref[...], hidden, preferred_element_type=jnp.float32)
    total += jnp.dot(scatter_ref[...], arrived_ref[...], preferred_element_type=jnp.float32)
    inverse = jnp.concatenate([inverse_ref[...]] * (width // inverse_ref.shape[1]), axis=1)
    mean = (total * inverse).astype(jnp.bfloat16)
    vectors = pack[width : width + PACK_ROWS, :].astype(jnp.float32)
    bias = vectors[0:1] + vectors[1:2]
    gain = vectors[2:3] + vectors[3:4]
    projected = jnp.dot(mean, pack[0:width, :], preferred_element_type=jnp.float32) + bias
    summed = hidden.astype(jnp.float32) + jnp.maximum(projected, 0.0)
    scale = lax.rsqrt(jnp.mean(summed * summed, axis=1, keepdims=True) + 1e-05)
    state = (summed * scale * gain).astype(jnp.bfloat16)
    state_ref, *refs = refs
    if step == layers - 1:
        state_ref[...] = state
        return
    outgoing_ref, *refs = refs
    state = jnp.where(step >= begin, state, hidden)
    state_ref[...] = state
    outgoing_ref[...] = jnp.dot(select_ref[...], state, preferred_element_type=jnp.float32).astype(jnp.bfloat16)
    for source_ref, target_ref in zip(passed_in, refs):
        target_ref[...] = source_ref[...]


def run_layer(step, layers, plane, hidden, arrived, tables, early, late, passed=()):
    outs = [jax.ShapeDtypeStruct(hidden.shape, jnp.bfloat16)]
    if step < layers - 1:
        outs.append(pltpu.VMEM(arrived.shape, jnp.bfloat16))
        outs += [jax.ShapeDtypeStruct(array.shape, jnp.bfloat16) for array in passed]
    return pl.pallas_call(
        functools.partial(layer_kernel, step, layers, len(passed)),
        out_shape=outs,
        in_specs=[SMEM] + [VMEM] * (8 + len(passed)),
        out_specs=[VMEM] * len(outs),
        compiler_params=PARAMS,
        name="layer",
    )(plane, hidden, arrived, *tables, early, late, *passed)


def local(features, weight, bias, gain, tile_col, tile_adj, send_rows, recv_dst):
    layers = lax.axis_size("layer")
    index = lax.axis_index("layer")
    peers, slots = send_rows.shape[2:]
    width = features.shape[-1]
    plane = index.reshape(1)
    order = [[i ^ FIRST for i in range(peers)]]
    core = (lax.axis_index("dom") % 2).reshape(1)
    span = (index % 2).reshape(1)
    cores = [[2 * chip, 2 * chip + 1] for chip in range(peers // 2)]
    down = [(z, (z - 1) % layers) for z in range(layers)]
    two_down = [(z, (z - 2) % layers) for z in range(layers)]
    send_rows = send_rows.transpose(0, 1, 3, 2)
    recv_dst = recv_dst.transpose(0, 1, 3, 2)

    outgoing, own_pack, own_half = first_gather(span, core, features, send_rows, weight, bias, gain)
    *tables, hidden = build_tables(span, tile_col, tile_adj, recv_dst, send_rows, features, outgoing)
    early = own_pack
    for step in range(layers - 1):
        arrived = lax.all_to_all(outgoing.reshape(peers, slots, width), "dom", 0, 0, axis_index_groups=order, tiled=True)
        arrived = arrived.reshape(peers * slots, width)
        if step == 0:
            half = lax.ppermute(own_half, "layer", down)
        late = lax.all_gather(half, "dom", axis_index_groups=cores, tiled=True)
        passed = []
        if step < layers - 2:
            source, pairs = (own_half, two_down) if step == 0 else (half, down)
            passed = [lax.ppermute(source, "layer", pairs)]
        hidden, outgoing, *more = run_layer(
            step, layers, plane, hidden, arrived, tables, early, late, passed
        )
        if more:
            half = more[0]
        if step == 0:
            first_state = hidden
        early = late
    last = layers - 1
    from_above = lax.ppermute(hidden, "layer", down[1:])

    def finish(outgoing, hidden):
        arrived = lax.all_to_all(outgoing.reshape(peers, slots, width), "dom", 0, 0, axis_index_groups=order, tiled=True)
        arrived = arrived.reshape(peers * slots, width)
        return run_layer(last, layers, plane, hidden, arrived, tables, early, own_pack)[0]

    def idle(outgoing, hidden):
        return jnp.zeros_like(hidden)

    state = lax.cond(index < last, finish, idle, outgoing, hidden)
    full = lax.ppermute(jnp.where(index == 0, state, from_above), "layer", down[:1])
    last_state = lax.cond(index == last, finish, idle, outgoing, hidden)
    own = jnp.where(index == 0, first_state, jnp.where(index == last, last_state, state))
    other = jnp.where(index == last, full, from_above)
    even = index % 2 == 0
    return jnp.stack([jnp.where(even, own, other), jnp.where(even, other, own)])[None]


def solution(mesh):
    in_specs = (
        P(None, "dom", None),
        P("layer", None, None),
        P("layer", None),
        P("layer", None),
        P(None, "dom", None),
        P(None, "dom", None, None, None),
        P(None, "dom", None, None),
        P(None, "dom", None, None),
    )
    out_specs = P("layer", None, "dom", None)
    return jax.shard_map(local, mesh=mesh, in_specs=in_specs, out_specs=out_specs, check_vma=False)
```

```python
import functools

import jax
import jax.numpy as jnp
from jax import lax
from jax.experimental import pallas as pl
from jax.experimental.pallas import tpu as pltpu
from jax.sharding import PartitionSpec as P

PACK_ROWS = 32
KERNEL_VMEM = 8 * 2**20
VMEM = pl.BlockSpec(memory_space=pltpu.VMEM)
SMEM = pl.BlockSpec(memory_space=pltpu.SMEM)
ANYWHERE = pl.BlockSpec(memory_space=pl.ANY)
PARAMS = pltpu.CompilerParams(vmem_limit_bytes=KERNEL_VMEM)
WIDE_PARAMS = pltpu.CompilerParams(vmem_limit_bytes=56 * 2**20)
CHUNKS = 4
FIRST, LATER = 40, 20


def slot_column(table, order):
    slots, count = table.shape
    rows = count * slots
    expand = (
        lax.broadcasted_iota(jnp.int32, (rows, count), 0) // slots
        == (lax.broadcasted_iota(jnp.int32, (rows, count), 1) ^ order)
    ).astype(jnp.bfloat16)
    spread = lax.dot_general(
        expand,
        table.astype(jnp.float32).astype(jnp.bfloat16),
        (((1,), (1,)), ((), ())),
        preferred_element_type=jnp.float32,
    )
    here = lax.broadcasted_iota(jnp.int32, (rows, slots), 0) % slots == lax.broadcasted_iota(
        jnp.int32, (rows, slots), 1
    )
    return jnp.sum(jnp.where(here, spread, 0.0), axis=1, keepdims=True)


def one_hot_rows(column, width):
    ids = lax.broadcasted_iota(jnp.int32, (column.shape[0], width), 1)
    return (column.astype(jnp.int32) == ids).astype(jnp.float32).astype(jnp.bfloat16)


def gather_out(select_ref, state, outgoing_ref, staged_ref, sems):
    size = select_ref.shape[0] // CHUNKS
    copies = []
    for chunk in range(CHUNKS):
        at = pl.ds(chunk * size, size)
        staged_ref[at, :] = jnp.dot(
            select_ref[at, :], state, preferred_element_type=jnp.float32
        ).astype(jnp.bfloat16)
        copies.append(pltpu.make_async_copy(staged_ref.at[at], outgoing_ref.at[at], sems.at[chunk]))
        copies[-1].start()
    for copy in copies:
        copy.wait()


def gather_scratch(slots, width):
    return [pltpu.VMEM((slots, width), jnp.bfloat16), pltpu.SemaphoreType.DMA((CHUNKS,))]


def pack_rows(weight_ref, bias_ref, gain_ref, pack_ref):
    width = weight_ref.shape[-1]
    pack_ref[0:width, :] = weight_ref[0]
    row = lax.broadcasted_iota(jnp.int32, (PACK_ROWS, width), 0)
    small = jnp.zeros((PACK_ROWS, width), jnp.float32)
    for at, ref in ((0, bias_ref), (2, gain_ref)):
        vector = ref[...]
        high = vector.astype(jnp.bfloat16).astype(jnp.float32)
        small = jnp.where(row == at, high, small)
        small = jnp.where(row == at + 1, vector - high, small)
    pack_ref[width : width + PACK_ROWS, :] = small.astype(jnp.bfloat16)


def first_kernel(
    span_ref,
    core_ref,
    features_ref,
    send_ref,
    weight_ref,
    bias_ref,
    gain_ref,
    outgoing_ref,
    own_ref,
    half_ref,
    select_ref,
    pack_ref,
    part_ref,
    pack_sems,
    staged_ref,
    sems,
):
    pack_rows(weight_ref, bias_ref, gain_ref, pack_ref)
    rows = part_ref.shape[0]
    part_ref[...] = jnp.where(core_ref[0] == 0, pack_ref[0:rows, :], pack_ref[rows : 2 * rows, :])
    copies = [
        pltpu.make_async_copy(part_ref, half_ref, pack_sems.at[0]),
        pltpu.make_async_copy(pack_ref, own_ref, pack_sems.at[1]),
    ]
    for copy in copies:
        copy.start()
    select_ref[...] = one_hot_rows(slot_column(send_ref[0, 0], FIRST), features_ref.shape[1])
    gather_out(select_ref, features_ref[0], outgoing_ref, staged_ref, sems)
    for copy in copies:
        copy.wait()


def first_gather(span, core, features, send_rows, weight, bias, gain):
    _, rows, width = features.shape
    slots, peers = send_rows.shape[2:]
    pack = (width + PACK_ROWS, width)
    half = (pack[0] // 2, width)
    return pl.pallas_call(
        first_kernel,
        grid_spec=pltpu.PrefetchScalarGridSpec(
            num_scalar_prefetch=2,
            grid=(1,),
            in_specs=[
                pl.BlockSpec((1, rows, width), lambda i, s, c: (s[0], 0, 0)),
                pl.BlockSpec((1, 1, slots, peers), lambda i, s, c: (s[0], 0, 0, 0)),
                pl.BlockSpec(weight.shape, lambda i, s, c: (0, 0, 0)),
                pl.BlockSpec(bias.shape, lambda i, s, c: (0, 0)),
                pl.BlockSpec(gain.shape, lambda i, s, c: (0, 0)),
            ],
            out_specs=[ANYWHERE] * 3,
            scratch_shapes=[
                pltpu.VMEM((peers * slots, rows), jnp.bfloat16),
                pltpu.VMEM(pack, jnp.bfloat16),
                pltpu.VMEM(half, jnp.bfloat16),
                pltpu.SemaphoreType.DMA((2,)),
            ]
            + gather_scratch(peers * slots, width),
        ),
        out_shape=[
            jax.ShapeDtypeStruct(shape, jnp.bfloat16) for shape in ((peers * slots, width), pack, half)
        ],
        compiler_params=WIDE_PARAMS,
        name="first_gather",
    )(span, core, features, send_rows, weight, bias, gain)


def tables_kernel(
    span_ref,
    col_ref,
    adj_ref,
    dest_ref,
    send_ref,
    features_ref,
    after_ref,
    scatter_ref,
    later_ref,
    near_ref,
    inverse_ref,
    select_ref,
    hidden_ref,
):
    hidden_ref[...] = features_ref[0]
    select_ref[...] = one_hot_rows(slot_column(send_ref[0, 0], LATER), hidden_ref.shape[0])
    _, blocks, tiles, side, _ = adj_ref.shape
    span = span_ref[0]
    rows = blocks * side
    for ref, order in ((scatter_ref, FIRST), (later_ref, LATER)):
        scatter = one_hot_rows(slot_column(dest_ref[0, 0], order), rows).astype(jnp.float32).T
        ref[...] = scatter.astype(jnp.bfloat16)
    degree = 1.0 + jnp.sum(scatter, axis=1, keepdims=True)
    for r in range(blocks):
        below = slice(r * side, (r + 1) * side)
        local_degree = jnp.zeros((side, 1), jnp.float32)
        for b in range(blocks):
            total = jnp.zeros((side, side), jnp.int32)
            for k in range(tiles):
                hit = col_ref[span, r, k] == b
                total += jnp.where(hit, adj_ref[0, r, k], 0)
            dense = total.astype(jnp.float32)
            local_degree += jnp.sum(dense, axis=1, keepdims=True)
            if b == r:
                dense += (
                    lax.broadcasted_iota(jnp.int32, (side, side), 0)
                    == lax.broadcasted_iota(jnp.int32, (side, side), 1)
                ).astype(jnp.float32)
            near_ref[below, b * side : (b + 1) * side] = dense.astype(jnp.bfloat16)
        inverse_ref[below, :] = jnp.broadcast_to(
            1.0 / (degree[below] + local_degree), (side, inverse_ref.shape[1])
        )


def build_tables(span, tile_col, tile_adj, recv_dst, send_rows, features, after):
    _, blocks, tiles, side, _ = tile_adj.shape
    _, rows, width = features.shape
    slots, peers = recv_dst.shape[2:]
    shapes = [
        ((rows, peers * slots), jnp.bfloat16),
        ((rows, peers * slots), jnp.bfloat16),
        ((rows, rows), jnp.bfloat16),
        ((rows, side), jnp.float32),
        ((peers * slots, rows), jnp.bfloat16),
        ((rows, width), jnp.bfloat16),
    ]
    return pl.pallas_call(
        tables_kernel,
        grid_spec=pltpu.PrefetchScalarGridSpec(
            num_scalar_prefetch=1,
            grid=(1,),
            in_specs=[
                SMEM,
                pl.BlockSpec((1, blocks, tiles, side, side), lambda i, s: (s[0], 0, 0, 0, 0)),
                pl.BlockSpec((1, 1, slots, peers), lambda i, s: (s[0], 0, 0, 0)),
                pl.BlockSpec((1, 1, slots, peers), lambda i, s: (s[0], 0, 0, 0)),
                pl.BlockSpec((1, rows, width), lambda i, s: (s[0], 0, 0)),
                ANYWHERE,
            ],
            out_specs=[pl.BlockSpec(shape, lambda i, s: (0, 0)) for shape, _ in shapes],
        ),
        out_shape=[jax.ShapeDtypeStruct(shape, dtype) for shape, dtype in shapes],
        compiler_params=PARAMS,
        name="build_tables",
    )(span, tile_col, tile_adj, recv_dst, send_rows, features, after)


def layer_kernel(
    step,
    layers,
    passed,
    plane_ref,
    hidden_ref,
    arrived_ref,
    near_ref,
    scatter_ref,
    inverse_ref,
    select_ref,
    early_ref,
    late_ref,
    *refs,
):
    passed_in, refs = refs[:passed], refs[passed:]
    rows, width = hidden_ref.shape
    plane = plane_ref[0]
    begin = jnp.where(plane == 0, 0, layers - 1 - plane)
    pack = jnp.where(plane == 0, early_ref[...], late_ref[...])
    hidden = hidden_ref[...]
    total = jnp.dot(near_ref[...], hidden, preferred_element_type=jnp.float32)
    total += jnp.dot(scatter_ref[...], arrived_ref[...], preferred_element_type=jnp.float32)
    inverse = jnp.concatenate([inverse_ref[...]] * (width // inverse_ref.shape[1]), axis=1)
    mean = (total * inverse).astype(jnp.bfloat16)
    vectors = pack[width : width + PACK_ROWS, :].astype(jnp.float32)
    bias = vectors[0:1] + vectors[1:2]
    gain = vectors[2:3] + vectors[3:4]
    projected = jnp.dot(mean, pack[0:width, :], preferred_element_type=jnp.float32) + bias
    summed = hidden.astype(jnp.float32) + jnp.maximum(projected, 0.0)
    scale = lax.rsqrt(jnp.mean(summed * summed, axis=1, keepdims=True) + 1e-05)
    state = (summed * scale * gain).astype(jnp.bfloat16)
    state_ref, *refs = refs
    if step == layers - 1:
        state_ref[...] = state
        return
    outgoing_ref, *refs = refs
    state = jnp.where(step >= begin, state, hidden)
    state_ref[...] = state
    outgoing_ref[...] = jnp.dot(select_ref[...], state, preferred_element_type=jnp.float32).astype(jnp.bfloat16)
    for source_ref, target_ref in zip(passed_in, refs):
        target_ref[...] = source_ref[...]


def run_layer(step, layers, plane, hidden, arrived, tables, early, late, passed=()):
    outs = [jax.ShapeDtypeStruct(hidden.shape, jnp.bfloat16)]
    if step < layers - 1:
        outs.append(pltpu.VMEM(arrived.shape, jnp.bfloat16))
        outs += [jax.ShapeDtypeStruct(array.shape, jnp.bfloat16) for array in passed]
    return pl.pallas_call(
        functools.partial(layer_kernel, step, layers, len(passed)),
        out_shape=outs,
        in_specs=[SMEM] + [VMEM] * (8 + len(passed)),
        out_specs=[VMEM] * len(outs),
        compiler_params=PARAMS,
        name="layer",
    )(plane, hidden, arrived, *tables, early, late, *passed)


def place_kernel(layers, plane_ref, first_ref, state_ref, last_ref, above_ref, out_ref, sems):
    plane = plane_ref[0]
    own, other = plane % 2, 1 - plane % 2

    def place(*moves):
        copies = [pltpu.make_async_copy(ref, out_ref.at[at], sems.at[i]) for i, (ref, at) in enumerate(moves)]
        for copy in copies:
            copy.start()
        for copy in copies:
            copy.wait()

    @pl.when(plane == 0)
    def _():
        place((first_ref, own), (above_ref, other))

    @pl.when((plane > 0) & (plane < layers - 1))
    def _():
        place((state_ref, own), (above_ref, other))

    @pl.when(plane == layers - 1)
    def _():
        place((last_ref, own))


def place_states(layers, plane, first, state, last, above):
    return pl.pallas_call(
        functools.partial(place_kernel, layers),
        out_shape=jax.ShapeDtypeStruct((2,) + state.shape, state.dtype),
        in_specs=[SMEM] + [ANYWHERE] * 4,
        out_specs=ANYWHERE,
        scratch_shapes=[pltpu.SemaphoreType.DMA((2,))],
        compiler_params=PARAMS,
        name="place_states",
    )(plane, first, state, last, above)


def full_kernel(layers, plane_ref, full_ref, before_ref, out_ref, sem):
    @pl.when(plane_ref[0] == layers - 1)
    def _():
        copy = pltpu.make_async_copy(full_ref, out_ref.at[layers % 2], sem)
        copy.start()
        copy.wait()


def place_full(layers, plane, full, out):
    return pl.pallas_call(
        functools.partial(full_kernel, layers),
        out_shape=jax.ShapeDtypeStruct(out.shape, out.dtype),
        in_specs=[SMEM] + [ANYWHERE] * 2,
        out_specs=ANYWHERE,
        scratch_shapes=[pltpu.SemaphoreType.DMA],
        input_output_aliases={2: 0},
        compiler_params=PARAMS,
        name="place_full",
    )(plane, full, out)


def local(features, weight, bias, gain, tile_col, tile_adj, send_rows, recv_dst):
    layers = lax.axis_size("layer")
    index = lax.axis_index("layer")
    peers, slots = send_rows.shape[2:]
    width = features.shape[-1]
    plane = index.reshape(1)
    orders = [[[i ^ order for i in range(peers)]] for order in (FIRST, LATER)]
    core = (lax.axis_index("dom") % 2).reshape(1)
    span = (index % 2).reshape(1)
    cores = [[2 * chip, 2 * chip + 1] for chip in range(peers // 2)]
    down = [(z, (z - 1) % layers) for z in range(layers)]
    two_down = [(z, (z - 2) % layers) for z in range(layers)]
    send_rows = send_rows.transpose(0, 1, 3, 2)
    recv_dst = recv_dst.transpose(0, 1, 3, 2)

    outgoing, own_pack, own_half = first_gather(span, core, features, send_rows, weight, bias, gain)
    *scatters, near, inverse, select, hidden = build_tables(span, tile_col, tile_adj, recv_dst, send_rows, features, outgoing)
    early = own_pack
    for step in range(layers - 1):
        arrived = lax.all_to_all(outgoing.reshape(peers, slots, width), "dom", 0, 0, axis_index_groups=orders[step > 0], tiled=True)
        arrived = arrived.reshape(peers * slots, width)
        tables = near, scatters[step > 0], inverse, select
        if step == 0:
            half = lax.ppermute(own_half, "layer", down)
        late = lax.all_gather(half, "dom", axis_index_groups=cores, tiled=True)
        passed = []
        if step < layers - 2:
            source, pairs = (own_half, two_down) if step == 0 else (half, down)
            passed = [lax.ppermute(source, "layer", pairs)]
        hidden, outgoing, *more = run_layer(
            step, layers, plane, hidden, arrived, tables, early, late, passed
        )
        if more:
            half = more[0]
        if step == 0:
            first_state = hidden
        early = late
    last = layers - 1
    from_above = lax.ppermute(hidden, "layer", down[1:])

    def finish(outgoing, hidden):
        arrived = lax.all_to_all(outgoing.reshape(peers, slots, width), "dom", 0, 0, axis_index_groups=orders[1], tiled=True)
        arrived = arrived.reshape(peers * slots, width)
        return run_layer(last, layers, plane, hidden, arrived, tables, early, own_pack)[0]

    def idle(outgoing, hidden):
        return jnp.zeros_like(hidden)

    state = lax.cond(index < last, finish, idle, outgoing, hidden)
    full = lax.ppermute(jnp.where(index == 0, state, from_above), "layer", down[:1])
    last_state = lax.cond(index == last, finish, idle, outgoing, hidden)
    out = place_states(layers, plane, first_state, state, last_state, from_above)
    return place_full(layers, plane, full, out)[None]


def solution(mesh):
    in_specs = (
        P(None, "dom", None),
        P("layer", None, None),
        P("layer", None),
        P("layer", None),
        P(None, "dom", None),
        P(None, "dom", None, None, None),
        P(None, "dom", None, None),
        P(None, "dom", None, None),
    )
    out_specs = P("layer", None, "dom", None)
    return jax.shard_map(local, mesh=mesh, in_specs=in_specs, out_specs=out_specs, check_vma=False)
```

```python
import functools

import jax
import jax.numpy as jnp
from jax import lax
from jax.experimental import pallas as pl
from jax.experimental.pallas import tpu as pltpu
from jax.sharding import PartitionSpec as P

PACK_ROWS = 32
KERNEL_VMEM = 8 * 2**20
VMEM = pl.BlockSpec(memory_space=pltpu.VMEM)
SMEM = pl.BlockSpec(memory_space=pltpu.SMEM)
ANYWHERE = pl.BlockSpec(memory_space=pl.ANY)
PARAMS = pltpu.CompilerParams(vmem_limit_bytes=KERNEL_VMEM)
WIDE_PARAMS = pltpu.CompilerParams(vmem_limit_bytes=56 * 2**20)
CHUNKS = 4
FIRST, LATER = 42, 20


def slot_column(table, order):
    slots, count = table.shape
    rows = count * slots
    expand = (
        lax.broadcasted_iota(jnp.int32, (rows, count), 0) // slots
        == (lax.broadcasted_iota(jnp.int32, (rows, count), 1) ^ order)
    ).astype(jnp.bfloat16)
    spread = lax.dot_general(
        expand,
        table.astype(jnp.float32).astype(jnp.bfloat16),
        (((1,), (1,)), ((), ())),
        preferred_element_type=jnp.float32,
    )
    here = lax.broadcasted_iota(jnp.int32, (rows, slots), 0) % slots == lax.broadcasted_iota(
        jnp.int32, (rows, slots), 1
    )
    return jnp.sum(jnp.where(here, spread, 0.0), axis=1, keepdims=True)


def one_hot_rows(column, width):
    ids = lax.broadcasted_iota(jnp.int32, (column.shape[0], width), 1)
    return (column.astype(jnp.int32) == ids).astype(jnp.float32).astype(jnp.bfloat16)


def gather_out(select_ref, state, outgoing_ref, staged_ref, sems):
    size = select_ref.shape[0] // CHUNKS
    copies = []
    for chunk in range(CHUNKS):
        at = pl.ds(chunk * size, size)
        staged_ref[at, :] = jnp.dot(
            select_ref[at, :], state, preferred_element_type=jnp.float32
        ).astype(jnp.bfloat16)
        copies.append(pltpu.make_async_copy(staged_ref.at[at], outgoing_ref.at[at], sems.at[chunk]))
        copies[-1].start()
    for copy in copies:
        copy.wait()


def gather_scratch(slots, width):
    return [pltpu.VMEM((slots, width), jnp.bfloat16), pltpu.SemaphoreType.DMA((CHUNKS,))]


def pack_rows(weight_ref, bias_ref, gain_ref, pack_ref):
    width = weight_ref.shape[-1]
    pack_ref[0:width, :] = weight_ref[0]
    row = lax.broadcasted_iota(jnp.int32, (PACK_ROWS, width), 0)
    small = jnp.zeros((PACK_ROWS, width), jnp.float32)
    for at, ref in ((0, bias_ref), (2, gain_ref)):
        vector = ref[...]
        high = vector.astype(jnp.bfloat16).astype(jnp.float32)
        small = jnp.where(row == at, high, small)
        small = jnp.where(row == at + 1, vector - high, small)
    pack_ref[width : width + PACK_ROWS, :] = small.astype(jnp.bfloat16)


def first_kernel(
    span_ref,
    core_ref,
    features_ref,
    send_ref,
    weight_ref,
    bias_ref,
    gain_ref,
    outgoing_ref,
    own_ref,
    half_ref,
    select_ref,
    pack_ref,
    part_ref,
    pack_sems,
    staged_ref,
    sems,
):
    pack_rows(weight_ref, bias_ref, gain_ref, pack_ref)
    rows = part_ref.shape[0]
    part_ref[...] = jnp.where(core_ref[0] == 0, pack_ref[0:rows, :], pack_ref[rows : 2 * rows, :])
    copies = [
        pltpu.make_async_copy(part_ref, half_ref, pack_sems.at[0]),
        pltpu.make_async_copy(pack_ref, own_ref, pack_sems.at[1]),
    ]
    for copy in copies:
        copy.start()
    select_ref[...] = one_hot_rows(slot_column(send_ref[0, 0], FIRST), features_ref.shape[1])
    gather_out(select_ref, features_ref[0], outgoing_ref, staged_ref, sems)
    for copy in copies:
        copy.wait()


def first_gather(span, core, features, send_rows, weight, bias, gain):
    _, rows, width = features.shape
    slots, peers = send_rows.shape[2:]
    pack = (width + PACK_ROWS, width)
    half = (pack[0] // 2, width)
    return pl.pallas_call(
        first_kernel,
        grid_spec=pltpu.PrefetchScalarGridSpec(
            num_scalar_prefetch=2,
            grid=(1,),
            in_specs=[
                pl.BlockSpec((1, rows, width), lambda i, s, c: (s[0], 0, 0)),
                pl.BlockSpec((1, 1, slots, peers), lambda i, s, c: (s[0], 0, 0, 0)),
                pl.BlockSpec(weight.shape, lambda i, s, c: (0, 0, 0)),
                pl.BlockSpec(bias.shape, lambda i, s, c: (0, 0)),
                pl.BlockSpec(gain.shape, lambda i, s, c: (0, 0)),
            ],
            out_specs=[ANYWHERE] * 3,
            scratch_shapes=[
                pltpu.VMEM((peers * slots, rows), jnp.bfloat16),
                pltpu.VMEM(pack, jnp.bfloat16),
                pltpu.VMEM(half, jnp.bfloat16),
                pltpu.SemaphoreType.DMA((2,)),
            ]
            + gather_scratch(peers * slots, width),
        ),
        out_shape=[
            jax.ShapeDtypeStruct(shape, jnp.bfloat16) for shape in ((peers * slots, width), pack, half)
        ],
        compiler_params=WIDE_PARAMS,
        name="first_gather",
    )(span, core, features, send_rows, weight, bias, gain)


def tables_kernel(
    span_ref,
    col_ref,
    adj_ref,
    dest_ref,
    send_ref,
    features_ref,
    after_ref,
    scatter_ref,
    later_ref,
    near_ref,
    inverse_ref,
    select_ref,
    hidden_ref,
):
    hidden_ref[...] = features_ref[0]
    select_ref[...] = one_hot_rows(slot_column(send_ref[0, 0], LATER), hidden_ref.shape[0])
    _, blocks, tiles, side, _ = adj_ref.shape
    span = span_ref[0]
    rows = blocks * side
    for ref, order in ((scatter_ref, FIRST), (later_ref, LATER)):
        scatter = one_hot_rows(slot_column(dest_ref[0, 0], order), rows).astype(jnp.float32).T
        ref[...] = scatter.astype(jnp.bfloat16)
    degree = 1.0 + jnp.sum(scatter, axis=1, keepdims=True)
    for r in range(blocks):
        below = slice(r * side, (r + 1) * side)
        local_degree = jnp.zeros((side, 1), jnp.float32)
        for b in range(blocks):
            total = jnp.zeros((side, side), jnp.int32)
            for k in range(tiles):
                hit = col_ref[span, r, k] == b
                total += jnp.where(hit, adj_ref[0, r, k], 0)
            dense = total.astype(jnp.float32)
            local_degree += jnp.sum(dense, axis=1, keepdims=True)
            if b == r:
                dense += (
                    lax.broadcasted_iota(jnp.int32, (side, side), 0)
                    == lax.broadcasted_iota(jnp.int32, (side, side), 1)
                ).astype(jnp.float32)
            near_ref[below, b * side : (b + 1) * side] = dense.astype(jnp.bfloat16)
        inverse_ref[below, :] = jnp.broadcast_to(
            1.0 / (degree[below] + local_degree), (side, inverse_ref.shape[1])
        )


def build_tables(span, tile_col, tile_adj, recv_dst, send_rows, features, after):
    _, blocks, tiles, side, _ = tile_adj.shape
    _, rows, width = features.shape
    slots, peers = recv_dst.shape[2:]
    shapes = [
        ((rows, peers * slots), jnp.bfloat16),
        ((rows, peers * slots), jnp.bfloat16),
        ((rows, rows), jnp.bfloat16),
        ((rows, side), jnp.float32),
        ((peers * slots, rows), jnp.bfloat16),
        ((rows, width), jnp.bfloat16),
    ]
    return pl.pallas_call(
        tables_kernel,
        grid_spec=pltpu.PrefetchScalarGridSpec(
            num_scalar_prefetch=1,
            grid=(1,),
            in_specs=[
                SMEM,
                pl.BlockSpec((1, blocks, tiles, side, side), lambda i, s: (s[0], 0, 0, 0, 0)),
                pl.BlockSpec((1, 1, slots, peers), lambda i, s: (s[0], 0, 0, 0)),
                pl.BlockSpec((1, 1, slots, peers), lambda i, s: (s[0], 0, 0, 0)),
                pl.BlockSpec((1, rows, width), lambda i, s: (s[0], 0, 0)),
                ANYWHERE,
            ],
            out_specs=[pl.BlockSpec(shape, lambda i, s: (0, 0)) for shape, _ in shapes],
        ),
        out_shape=[jax.ShapeDtypeStruct(shape, dtype) for shape, dtype in shapes],
        compiler_params=PARAMS,
        name="build_tables",
    )(span, tile_col, tile_adj, recv_dst, send_rows, features, after)


def layer_kernel(
    step,
    layers,
    passed,
    plane_ref,
    hidden_ref,
    arrived_ref,
    near_ref,
    scatter_ref,
    inverse_ref,
    select_ref,
    early_ref,
    late_ref,
    *refs,
):
    passed_in, refs = refs[:passed], refs[passed:]
    rows, width = hidden_ref.shape
    plane = plane_ref[0]
    begin = jnp.where(plane == 0, 0, layers - 1 - plane)
    pack = jnp.where(plane == 0, early_ref[...], late_ref[...])
    hidden = hidden_ref[...]
    total = jnp.dot(near_ref[...], hidden, preferred_element_type=jnp.float32)
    total += jnp.dot(scatter_ref[...], arrived_ref[...], preferred_element_type=jnp.float32)
    inverse = jnp.concatenate([inverse_ref[...]] * (width // inverse_ref.shape[1]), axis=1)
    mean = (total * inverse).astype(jnp.bfloat16)
    vectors = pack[width : width + PACK_ROWS, :].astype(jnp.float32)
    bias = vectors[0:1] + vectors[1:2]
    gain = vectors[2:3] + vectors[3:4]
    projected = jnp.dot(mean, pack[0:width, :], preferred_element_type=jnp.float32) + bias
    summed = hidden.astype(jnp.float32) + jnp.maximum(projected, 0.0)
    scale = lax.rsqrt(jnp.mean(summed * summed, axis=1, keepdims=True) + 1e-05)
    state = (summed * scale * gain).astype(jnp.bfloat16)
    state_ref, *refs = refs
    if step == layers - 1:
        state_ref[...] = state
        return
    outgoing_ref, *refs = refs
    state = jnp.where(step >= begin, state, hidden)
    state_ref[...] = state
    outgoing_ref[...] = jnp.dot(select_ref[...], state, preferred_element_type=jnp.float32).astype(jnp.bfloat16)
    for source_ref, target_ref in zip(passed_in, refs):
        target_ref[...] = source_ref[...]


def run_layer(step, layers, plane, hidden, arrived, tables, early, late, passed=()):
    outs = [jax.ShapeDtypeStruct(hidden.shape, jnp.bfloat16)]
    if step < layers - 1:
        outs.append(pltpu.VMEM(arrived.shape, jnp.bfloat16))
        outs += [jax.ShapeDtypeStruct(array.shape, jnp.bfloat16) for array in passed]
    return pl.pallas_call(
        functools.partial(layer_kernel, step, layers, len(passed)),
        out_shape=outs,
        in_specs=[SMEM] + [VMEM] * (8 + len(passed)),
        out_specs=[VMEM] * len(outs),
        compiler_params=PARAMS,
        name="layer",
    )(plane, hidden, arrived, *tables, early, late, *passed)


def place_kernel(layers, plane_ref, first_ref, state_ref, last_ref, above_ref, out_ref, sems):
    plane = plane_ref[0]
    own, other = plane % 2, 1 - plane % 2

    def place(*moves):
        copies = [pltpu.make_async_copy(ref, out_ref.at[at], sems.at[i]) for i, (ref, at) in enumerate(moves)]
        for copy in copies:
            copy.start()
        for copy in copies:
            copy.wait()

    @pl.when(plane == 0)
    def _():
        place((first_ref, own), (above_ref, other))

    @pl.when((plane > 0) & (plane < layers - 1))
    def _():
        place((state_ref, own), (above_ref, other))

    @pl.when(plane == layers - 1)
    def _():
        place((last_ref, own))


def place_states(layers, plane, first, state, last, above):
    return pl.pallas_call(
        functools.partial(place_kernel, layers),
        out_shape=jax.ShapeDtypeStruct((2,) + state.shape, state.dtype),
        in_specs=[SMEM] + [ANYWHERE] * 4,
        out_specs=ANYWHERE,
        scratch_shapes=[pltpu.SemaphoreType.DMA((2,))],
        compiler_params=PARAMS,
        name="place_states",
    )(plane, first, state, last, above)


def full_kernel(layers, plane_ref, full_ref, before_ref, out_ref, sem):
    @pl.when(plane_ref[0] == layers - 1)
    def _():
        copy = pltpu.make_async_copy(full_ref, out_ref.at[layers % 2], sem)
        copy.start()
        copy.wait()


def place_full(layers, plane, full, out):
    return pl.pallas_call(
        functools.partial(full_kernel, layers),
        out_shape=jax.ShapeDtypeStruct(out.shape, out.dtype),
        in_specs=[SMEM] + [ANYWHERE] * 2,
        out_specs=ANYWHERE,
        scratch_shapes=[pltpu.SemaphoreType.DMA],
        input_output_aliases={2: 0},
        compiler_params=PARAMS,
        name="place_full",
    )(plane, full, out)


def local(features, weight, bias, gain, tile_col, tile_adj, send_rows, recv_dst):
    layers = lax.axis_size("layer")
    index = lax.axis_index("layer")
    peers, slots = send_rows.shape[2:]
    width = features.shape[-1]
    plane = index.reshape(1)
    orders = [[[i ^ order for i in range(peers)]] for order in (FIRST, LATER)]
    core = (lax.axis_index("dom") % 2).reshape(1)
    span = (index % 2).reshape(1)
    cores = [[2 * chip, 2 * chip + 1] for chip in range(peers // 2)]
    down = [(z, (z - 1) % layers) for z in range(layers)]
    two_down = [(z, (z - 2) % layers) for z in range(layers)]
    send_rows = send_rows.transpose(0, 1, 3, 2)
    recv_dst = recv_dst.transpose(0, 1, 3, 2)

    outgoing, own_pack, own_half = first_gather(span, core, features, send_rows, weight, bias, gain)
    *scatters, near, inverse, select, hidden = build_tables(span, tile_col, tile_adj, recv_dst, send_rows, features, outgoing)
    early = own_pack
    for step in range(layers - 1):
        arrived = lax.all_to_all(outgoing.reshape(peers, slots, width), "dom", 0, 0, axis_index_groups=orders[step > 0], tiled=True)
        arrived = arrived.reshape(peers * slots, width)
        tables = near, scatters[step > 0], inverse, select
        if step == 0:
            half = lax.ppermute(own_half, "layer", down)
        late = lax.all_gather(half, "dom", axis_index_groups=cores, tiled=True)
        passed = []
        if step < layers - 2:
            source, pairs = (own_half, two_down) if step == 0 else (half, down)
            passed = [lax.ppermute(source, "layer", pairs)]
        hidden, outgoing, *more = run_layer(
            step, layers, plane, hidden, arrived, tables, early, late, passed
        )
        if more:
            half = more[0]
        if step == 0:
            first_state = hidden
        early = late
    last = layers - 1
    from_above = lax.ppermute(hidden, "layer", down[1:])

    def finish(outgoing, hidden):
        arrived = lax.all_to_all(outgoing.reshape(peers, slots, width), "dom", 0, 0, axis_index_groups=orders[1], tiled=True)
        arrived = arrived.reshape(peers * slots, width)
        return run_layer(last, layers, plane, hidden, arrived, tables, early, own_pack)[0]

    def idle(outgoing, hidden):
        return jnp.zeros_like(hidden)

    state = lax.cond(index < last, finish, idle, outgoing, hidden)
    full = lax.ppermute(jnp.where(index == 0, state, from_above), "layer", down[:1])
    last_state = lax.cond(index == last, finish, idle, outgoing, hidden)
    out = place_states(layers, plane, first_state, state, last_state, from_above)
    return place_full(layers, plane, full, out)[None]


def solution(mesh):
    in_specs = (
        P(None, "dom", None),
        P("layer", None, None),
        P("layer", None),
        P("layer", None),
        P(None, "dom", None),
        P(None, "dom", None, None, None),
        P(None, "dom", None, None),
        P(None, "dom", None, None),
    )
    out_specs = P("layer", None, "dom", None)
    return jax.shard_map(local, mesh=mesh, in_specs=in_specs, out_specs=out_specs, check_vma=False)
```
